256 devices in a mesh: ctx: 16 (over z, core), row: 4 (over x), col: 4 (over y).
Axes of the slice: x: 4, y: 4, z: 8, core: 2. Of those that a mesh axis runs over, the one named last changes fastest.
Arguments:
- projected: bfloat16 [16384, 8704], P(('ctx', 'row'), 'col'), may hold values from -6 to 6
- conv_taps: float32 [3, 8704], P(None, 'col'), may hold values from -3 to 3
- out_weight: bfloat16 [8192, 8192], P('col', 'row'), may hold values from -0.0625 to 0.0625
Outputs:
- output: bfloat16 [16384, 8192], P(('ctx', 'col'), 'row')
The draws below stay inside these ranges and needn't reach their ends.
All inputs are finite; a program needn't handle non-finite values.
Results may differ from the reference program's by a relative error of at most 0.02.
Values may be sent and summed in bfloat16 or wider, within the bound.
A program may use at most 192 MiB of HBM per device.

```python
import jax
import jax.numpy as jnp
import numpy as np
from jax import lax

D = 8192
H = 16
FEAT = 16
DV = 512
TAPS = 3
TOK_DEV = 256
PHI = 153
HG = 4
TOKENS = 16384


def draw_conv_taps(key, part):
    channel_width = 2 * FEAT + DV
    channels = H * channel_width
    inside = jnp.arange(channels, dtype=jnp.int32) % channel_width
    is_value = inside >= 2 * FEAT
    first_key, second_key = jax.random.split(jax.random.fold_in(key, 11))
    tap_rows = jnp.clip(0.6 * jax.random.normal(first_key, (TAPS, channels), jnp.float32), -3.0, 3.0)
    small_lead = jax.random.uniform(second_key, (channels,), jnp.float32, -0.04, 0.04)
    leading = jnp.where(is_value, small_lead, tap_rows[0])
    return jnp.concatenate([leading[None], tap_rows[1:]], axis=0)


def shard_levels(own_key, dims, shards, low, top_value):
    def one(axis_at, blocks):
        steps = jax.random.uniform(jax.random.fold_in(jax.random.fold_in(own_key, 6), axis_at), (blocks,), jnp.float32, low / len(shards), top_value / len(shards))
        return jnp.repeat(jnp.exp(steps), dims[axis_at] // blocks).reshape((-1,) + (1,) * (len(dims) - axis_at - 1))

    loudness = one(*shards[0])
    for cut in shards[1:]:
        loudness = loudness * one(*cut)
    return loudness


def scatter_about(rng, extent, deviation, limit, pieces=(), held_as=jnp.bfloat16):
    array = deviation * jax.random.normal(rng, extent, jnp.float32)
    if pieces:
        array = array * shard_levels(rng, extent, pieces, -0.22, 0.18)
    return jnp.clip(array, -limit, limit).astype(held_as)


def setup_inputs(seed: int = 0) -> dict:
    key_of = jax.random.split(jax.random.key(seed), 4)
    return {
        "projected": scatter_about(key_of[0], (TOKENS, H * (2 * FEAT + DV)), 1.0, 6.0, ((0, 64), (1, 4))),
        "conv_taps": draw_conv_taps(jax.random.fold_in(key_of[3], 71), 0),
        "out_weight": scatter_about(key_of[2], (H * DV, D), (H * DV) ** -0.5, 0.0625, ((0, 4), (1, 4))),
    }


def features(values):
    width = values.shape[-1]
    first, second = np.triu_indices(width)
    coef = np.where(first == second, (2.0 * width) ** -0.5, width ** -0.5).astype(np.float32)
    ones = jnp.ones(values.shape[:-1] + (1,), values.dtype)
    quad = values[..., first] * values[..., second] * coef
    return jnp.concatenate([ones, values * (width ** -0.25), quad], axis=-1)


def reference(projected, conv_taps, out_weight):
    blocks = TOKENS // TOK_DEV
    width = 2 * FEAT + DV
    group_cols = HG * DV
    proj_blocks = projected.reshape(blocks, TOK_DEV, H * width)
    causal = jnp.arange(TOK_DEV)[:, None] >= jnp.arange(TOK_DEV)[None, :]
    init = (jnp.zeros((2, H * width), jnp.bfloat16), jnp.zeros((H, PHI, DV), jnp.float32), jnp.zeros((H, PHI), jnp.float32))

    def step(carry, block):
        tail, state_num, state_den = carry
        extended = jnp.concatenate([tail, block], axis=0).astype(jnp.float32)
        convolved = conv_taps[0] * extended[2:] + conv_taps[1] * extended[1:-1] + conv_taps[2] * extended[:-2]
        gated = (extended[2:] * convolved).astype(jnp.bfloat16).reshape(TOK_DEV, H, width)
        query = gated[..., :FEAT].astype(jnp.float32)
        key = gated[..., FEAT:2 * FEAT].astype(jnp.float32)
        value = gated[..., 2 * FEAT:].astype(jnp.float32)
        scores = jnp.einsum('thi,shi->hts', query, key) * (FEAT ** -0.5)
        kernel = jnp.where(causal[None], 1.0 + scores + 0.5 * scores * scores, 0.0).astype(jnp.bfloat16).astype(jnp.float32)
        num_in = jnp.einsum('hts,shd->thd', kernel, value)
        den_in = jnp.sum(kernel, axis=-1).T
        phi_query = features(query)
        phi_key = features(key)
        num_out = jnp.einsum('thf,hfd->thd', phi_query, state_num, precision=lax.Precision.HIGHEST)
        den_out = jnp.einsum('thf,hf->th', phi_query, state_den, precision=lax.Precision.HIGHEST)
        attended = ((num_out + num_in) / (den_out + den_in)[..., None]).astype(jnp.bfloat16).reshape(TOK_DEV, H * DV)
        new_num = state_num + jnp.einsum('thf,thd->hfd', phi_key, value, precision=lax.Precision.HIGHEST)
        new_den = state_den + jnp.sum(phi_key, axis=0)
        total = jnp.zeros((TOK_DEV, D), jnp.float32)
        for group in range(H // HG):
            lower = group * group_cols
            partial_out = jnp.dot(attended[:, lower:lower + group_cols], out_weight[lower:lower + group_cols], preferred_element_type=jnp.float32).astype(jnp.bfloat16)
            total = total + lax.optimization_barrier(partial_out).astype(jnp.float32)
        return (block[-2:], new_num, new_den), total.astype(jnp.bfloat16)

    final, outs = lax.scan(step, init, proj_blocks)
    return outs.reshape(TOKENS, D)
```

```python
import jax
import jax.numpy as jnp
import numpy as np
from jax import lax
from jax.experimental import pallas as pl
from jax.experimental.pallas import tpu as pltpu
from jax.sharding import PartitionSpec as P

MESH = pl.DeviceIdType.MESH
FEAT = 16
DV = 512
PHI = 153
WIN = 640
BLK = 256
ROWS = 4
CTX = 16
TOK = ROWS * BLK
FP = 256
FS = 192
SR, SC = 48, 128
K = 8
T = BLK // K
CH = 4 * T
HALF = 1024
Q0, K0 = 96, 112
F32, BF16 = jnp.float32, jnp.bfloat16
NT = (((1,), (1,)), ((), ()))


def selectors():
    first, second = np.triu_indices(FEAT)
    k1, k2, q1, q2 = (np.zeros((128, FP), np.float32) for _ in range(4))
    for m in (k1, k2, q1, q2):
        m[0, 0] = 1.0
    for i in range(FEAT):
        k1[K0 + i, 1 + i] = 1.0
        k2[0, 1 + i] = 1.0
        q1[Q0 + i, 1 + i] = 1.0
        q2[0, 1 + i] = 0.25
    for n, (i, j) in enumerate(zip(first, second)):
        at = 1 + FEAT + n
        k1[K0 + i, at] = 1.0
        k2[K0 + j, at] = 1.0
        q1[Q0 + i, at] = 1.0
        q2[Q0 + j, at] = 1.0 / 32 if i == j else 1.0 / 16
    move = np.zeros((128, 128), np.float32)
    for i in range(FEAT):
        move[Q0 + i, K0 + i] = 0.25
    return k1.T, k2.T, q1, q2, move


def dot(a, b):
    return jnp.dot(a, b, preferred_element_type=F32)


def dot_nt(a, b):
    return lax.dot_general(a, b, NT, preferred_element_type=F32)


def kernel(
    proj, taps, weight, k1, k2, q1, q2, move, out,
    raw, gated, num, den, phiq, inner, mine, z1, z2, outer, w, att, part, own, opp, left_in, right_in,
    xs, xr, ts, tr, ws, z1s, z1r, z2s, z2r, ags, agr, rss, rsr,
):
    c, h, g = lax.axis_index("ctx"), lax.axis_index("row"), lax.axis_index("col")

    def at(axis, index, by, n):
        return {axis: lax.rem(index + by, n)}

    def row(by):
        return at("row", h, by, ROWS)

    def ctx(by):
        return at("ctx", c, by, CTX)

    right, left = at("col", g, 1, 4), at("col", g, 3, 4)
    sends_tail = jnp.logical_and(h == ROWS - 1, c < CTX - 1)

    load_w = pltpu.make_async_copy(weight, w, ws)
    load_w.start()

    bar = pltpu.get_barrier_semaphore()

    def greet(where):
        pl.semaphore_signal(bar, inc=1, device_id=where, device_id_type=MESH)

    for i in range(1, ROWS):
        greet(row(i))

    @pl.loop(1, CTX)
    def _(i):
        greet(ctx(i))

    greet(right)
    greet(left)

    @pl.when(jnp.logical_and(h != ROWS - 1, c > 0))
    def _():
        greet({"ctx": c - 1, "row": ROWS - 1})

    pl.semaphore_wait(bar, ROWS - 1 + CTX - 1 + 2 + jnp.where(sends_tail, ROWS - 1, 0))

    def window(head):
        return pl.ds(pl.multiple_of(head * DV, DV), WIN)

    def exchange(i):
        return pltpu.make_async_remote_copy(
            proj.at[:, window(lax.rem(h + i, ROWS))],
            raw.at[pl.ds(pl.multiple_of(16 + h * BLK, 16), BLK)],
            xs.at[i],
            xr.at[i],
            row(i),
            MESH,
        )

    def tail(head):
        return pltpu.make_async_remote_copy(
            proj.at[pl.ds(BLK - 16, 16), pl.ds(head * DV, WIN)],
            raw.at[pl.ds(0, 16)],
            ts.at[head],
            tr,
            {"ctx": lax.rem(c + 1, CTX), "row": head},
            MESH,
        )

    for i in (2, 1, 3):
        exchange(i).start()

    @pl.when(sends_tail)
    def _():
        for head in range(ROWS):
            tail(head).start()

    keep = pltpu.make_async_copy(
        proj.at[:, window(h)], raw.at[pl.ds(pl.multiple_of(16 + h * BLK, 16), BLK)], xs.at[0]
    )
    keep.start()
    keep.wait()

    @pl.when(c == 0)
    def _():
        raw[pl.ds(0, 16), :] = jnp.zeros((16, WIN), BF16)

    @pl.when(c > 0)
    def _():
        tail(0).wait_recv()

    for i in (1, 3, 2):
        exchange(i).wait_recv()

    tap = taps[:, window(h)]
    lane = lax.broadcasted_iota(jnp.int32, (BLK, 128), 1)
    feature = lax.broadcasted_iota(jnp.int32, (FS, DV), 0)
    ones = jnp.ones((8, BLK), BF16)
    inner[...] = jnp.zeros((FS, DV), F32)

    @pl.loop(0, ROWS)
    def _(b):
        x = raw[pl.ds(pl.multiple_of(b * BLK, 16), BLK + 16), :].astype(F32)
        y = x * (tap[0:1] * x + tap[1:2] * pltpu.roll(x, 1, 0) + tap[2:3] * pltpu.roll(x, 2, 0))
        y = pltpu.roll(y[16:], WIN - 2 * FEAT * (h + 1), 1)
        rows = pl.ds(pl.multiple_of(b * BLK, BLK), BLK)
        value = y[:, :DV].astype(BF16)
        qk = jnp.where(lane == 0, 1.0, y[:, DV:]).astype(BF16)
        gated[rows, :DV] = value
        gated[rows, DV:] = qk
        phik = (dot_nt(k1[...], qk) * dot_nt(k2[...], qk)).astype(BF16)
        total = dot_nt(ones, phik)[0:1]
        total = jnp.concatenate([total, jnp.zeros((1, DV - FP), F32)], axis=1)
        state = jnp.where(feature == PHI, total, dot(phik[:FS], value))
        before = inner[...]
        mine[b] = before.astype(BF16)
        inner[...] = before + state

    mine[ROWS] = inner[...].astype(BF16)

    def share(index):
        return (
            pl.ds(pl.multiple_of(lax.div(index, 4) * SR, SR), SR),
            pl.ds(pl.multiple_of(lax.rem(index, 4) * SC, SC), SC),
        )

    def to_owner(i):
        r, s = share(lax.rem(c + i, CTX))
        return pltpu.make_async_remote_copy(
            mine.at[ROWS, r, s], z1.at[c], z1s.at[i], z1r.at[i], ctx(i), MESH
        )

    def from_owner(i):
        r, s = share(c)
        return pltpu.make_async_remote_copy(
            z2.at[lax.rem(c + i, CTX)], outer.at[r, s], z2s.at[i], z2r.at[i], ctx(i), MESH
        )

    @pl.loop(1, CTX)
    def _(i):
        to_owner(i).start()

    r, s = share(c)
    z1[c] = mine[ROWS, r, s]
    outer[FS:, :] = jnp.zeros((FP - FS, DV), BF16)

    causal = lax.broadcasted_iota(jnp.int32, (BLK, BLK), 0) >= lax.broadcasted_iota(
        jnp.int32, (BLK, BLK), 1
    )

    @pl.loop(0, ROWS)
    def _(b):
        rows = pl.ds(pl.multiple_of(b * BLK, BLK), BLK)
        qk = gated[rows, DV:]
        value = gated[rows, :DV]
        phi = (dot(qk, q1[...]) * dot(qk, q2[...])).astype(BF16)
        phiq[rows, :] = phi
        z = dot_nt(dot(qk, move[...]).astype(BF16), qk)
        kern = jnp.where(causal, 1.0 + z + 0.5 * z * z, 0.0).astype(BF16)
        prior = mine[b]
        prior_total = prior[PHI : PHI + 1, :FP].astype(F32)
        num[rows, :] = dot(kern, value) + dot(phi[:, :FS], prior)
        weight_sum = jnp.sum(kern.astype(F32), axis=1, keepdims=True) + jnp.sum(
            phi.astype(F32) * prior_total, axis=1, keepdims=True
        )
        den[rows, :] = jnp.broadcast_to(weight_sum, (BLK, 128))

    @pl.loop(1, CTX)
    def _(i):
        to_owner(i).wait_recv()

    run = jnp.zeros((SR, SC), F32)
    for i in range(CTX):
        z2[i] = run.astype(BF16)
        run = run + z1[i].astype(F32)

    @pl.loop(1, CTX)
    def _(i):
        from_owner(i).start()

    r, s = share(c)
    outer[r, s] = z2[c]

    @pl.loop(1, CTX)
    def _(i):
        from_owner(i).wait_recv()

    load_w.wait()

    def head(by):
        return pl.ds(pl.multiple_of(lax.rem(h + by, ROWS) * DV, DV), DV)

    def ag(k, which):
        rows, of, to = (
            (pl.ds(0, CH), 0, 1),
            (pl.ds(0, CH), 0, 3),
            (pl.ds(0, CH // 2), 3, 1),
            (pl.ds(CH // 2, CH // 2), 1, 3),
        )[which]
        return pltpu.make_async_remote_copy(
            att.at[k, rows, head(of)],
            att.at[k, rows, head(of)],
            ags.at[k, which],
            agr.at[k, which],
            row(to),
            MESH,
        )

    def rs(k, which):
        a, b = pl.ds(0, HALF), pl.ds(HALF, HALF)
        j, cols, land, to = (
            (2, a, opp.at[k, 0], right),
            (2, b, opp.at[k, 1], left),
            (1, b, left_in.at[k, :, b], right),
            (3, a, right_in.at[k, :, a], left),
            (1, a, left_in.at[k, :, a], right),
            (3, b, right_in.at[k, :, b], left),
        )[which]
        return pltpu.make_async_remote_copy(
            part.at[k, pl.ds(j * T, T), cols], land, rss.at[k, which], rsr.at[k, which], to, MESH
        )

    outer_total = outer[PHI : PHI + 1, :FP].astype(F32)

    @pl.loop(0, K + 4)
    def _(step):
        @pl.when(step < K)
        def _():
            k = step
            spots = [
                pl.ds(pl.multiple_of(lax.rem(g + j, ROWS) * BLK + k * T, T), T) for j in range(4)
            ]
            phi = jnp.concatenate([phiq[spot, :] for spot in spots], axis=0)
            top = jnp.concatenate([num[spot, :] for spot in spots], axis=0) + dot(phi, outer[...])
            bottom = jnp.concatenate([den[spot, :] for spot in spots], axis=0)[:, 0:1] + jnp.sum(
                phi.astype(F32) * outer_total, axis=1, keepdims=True
            )
            att[k, :, head(0)] = (top / bottom).astype(BF16)
            ag(k, 0).start()
            ag(k, 1).start()

        @pl.when(jnp.logical_and(step >= 1, step < K + 1))
        def _():
            k = step - 1
            ag(k, 0).wait_recv()
            ag(k, 2).start()
            ag(k, 1).wait_recv()
            ag(k, 3).start()

        @pl.when(jnp.logical_and(step >= 2, step < K + 2))
        def _():
            k = step - 2
            ag(k, 2).wait_recv()
            ag(k, 3).wait_recv()
            for half in range(2):
                for n in range(2):
                    cols = slice(half * HALF + n * 512, half * HALF + n * 512 + 512)
                    p = dot(att[k], w[:, cols])
                    own[k, :, cols] = p[:T]
                    part[k, T:, cols] = p[T:].astype(BF16)
                for which in ((0, 3), (1, 2))[half]:
                    rs(k, which).start()

        @pl.when(jnp.logical_and(step >= 3, step < K + 3))
        def _():
            k = step - 3
            rs(k, 0).wait_recv()
            part[k, T : 2 * T, :HALF] = (
                part[k, T : 2 * T, :HALF].astype(F32) + opp[k, 0].astype(F32)
            ).astype(BF16)
            rs(k, 4).start()
            rs(k, 1).wait_recv()
            part[k, 3 * T :, HALF:] = (
                part[k, 3 * T :, HALF:].astype(F32) + opp[k, 1].astype(F32)
            ).astype(BF16)
            rs(k, 5).start()

        @pl.when(step >= 4)
        def _():
            k = step - 4
            for which in range(2, 6):
                rs(k, which).wait_recv()
            out[pl.ds(pl.multiple_of(k * T, T), T), :] = (
                own[k] + left_in[k].astype(F32) + right_in[k].astype(F32)
            ).astype(BF16)

    for i in (1, 2, 3):
        exchange(i).wait_send()

    @pl.when(sends_tail)
    def _():
        for one in range(ROWS):
            tail(one).wait_send()

    @pl.loop(1, CTX)
    def _(i):
        to_owner(i).wait_send()
        from_owner(i).wait_send()

    @pl.loop(0, K)
    def _(k):
        for which in range(4):
            ag(k, which).wait_send()
        for which in range(6):
            rs(k, which).wait_send()


def shards(projected, conv_taps, out_weight):
    constants = [jnp.asarray(m, BF16) for m in selectors()]
    vmem = pl.BlockSpec(memory_space=pltpu.VMEM)
    hbm = pl.BlockSpec(memory_space=pl.ANY)
    dma = pltpu.SemaphoreType.DMA
    return pl.pallas_call(
        kernel,
        out_shape=jax.ShapeDtypeStruct((BLK, 2048), BF16),
        in_specs=[hbm, vmem, hbm] + [vmem] * 5,
        out_specs=vmem,
        scratch_shapes=[
            pltpu.VMEM((16 + TOK, WIN), BF16),
            pltpu.VMEM((TOK, WIN), BF16),
            pltpu.VMEM((TOK, DV), F32),
            pltpu.VMEM((TOK, 128), F32),
            pltpu.VMEM((TOK, FP), BF16),
            pltpu.VMEM((FS, DV), F32),
            pltpu.VMEM((ROWS + 1, FS, DV), BF16),
            pltpu.VMEM((CTX, SR, SC), BF16),
            pltpu.VMEM((CTX, SR, SC), BF16),
            pltpu.VMEM((FP, DV), BF16),
            pltpu.VMEM((2048, 2048), BF16),
            pltpu.VMEM((K, CH, 2048), BF16),
            pltpu.VMEM((K, CH, 2048), BF16),
            pltpu.VMEM((K, T, 2048), F32),
            pltpu.VMEM((K, 2, T, HALF), BF16),
            pltpu.VMEM((K, T, 2048), BF16),
            pltpu.VMEM((K, T, 2048), BF16),
            dma((4,)),
            dma((4,)),
            dma((4,)),
            dma,
            dma,
            dma((CTX,)),
            dma((CTX,)),
            dma((CTX,)),
            dma((CTX,)),
            dma((K, 4)),
            dma((K, 4)),
            dma((K, 6)),
            dma((K, 6)),
        ],
        compiler_params=pltpu.CompilerParams(
            collective_id=0, has_side_effects=True, vmem_limit_bytes=56 * 2**20
        ),
    )(projected, conv_taps, out_weight, *constants)


def solution(mesh):
    in_specs = (P(("ctx", "row"), "col"), P(None, "col"), P("col", "row"))
    out_specs = P(("ctx", "col"), "row")
    return jax.shard_map(shards, mesh=mesh, in_specs=in_specs, out_specs=out_specs, check_vma=False)
```

```python
import jax
import jax.numpy as jnp
import numpy as np
from jax import lax
from jax.experimental import pallas as pl
from jax.experimental.pallas import tpu as pltpu
from jax.sharding import PartitionSpec as P

MESH = pl.DeviceIdType.MESH
FEAT = 16
DV = 512
PHI = 153
WIN = 640
BLK = 256
ROWS = 4
CTX = 16
TOK = ROWS * BLK
FP = 256
FS = 192
SR, SC = 48, 128
TILES = 5
K = 8
T = BLK // K
CH = 4 * T
HALF = 1024
Q0, K0 = 96, 112
F32, BF16 = jnp.float32, jnp.bfloat16
NT = (((1,), (1,)), ((), ()))


def selectors():
    first, second = np.triu_indices(FEAT)
    k1, k2, q1, q2 = (np.zeros((FP, 128), np.float32) for _ in range(4))
    for m in (k1, k2, q1, q2):
        m[0, 0] = 1.0
    for i in range(FEAT):
        k1[1 + i, K0 + i] = 1.0
        k2[1 + i, 0] = 1.0
        q1[1 + i, Q0 + i] = 1.0
        q2[1 + i, 0] = 0.25
    for n, (i, j) in enumerate(zip(first, second)):
        at = 1 + FEAT + n
        k1[at, K0 + i] = 1.0
        k2[at, K0 + j] = 1.0
        q1[at, Q0 + i] = 1.0
        q2[at, Q0 + j] = 1.0 / 32 if i == j else 1.0 / 16
    move = np.zeros((128, 128), np.float32)
    for i in range(FEAT):
        move[K0 + i, Q0 + i] = 0.25
    return np.concatenate([k1, k2, q1, q2, move])


def dot(a, b):
    return jnp.dot(a, b, preferred_element_type=F32)


def dot_nt(a, b):
    return lax.dot_general(a, b, NT, preferred_element_type=F32)


def kernel(
    proj, taps, weight, select, out,
    x, packed, quarter, raw, land, tap, gated, phik, totals, num, den, phiq,
    inner, mine, z1, z2, outer, w, att, part, own, opp, left_in, right_in,
    ps, xs, xr, ts, tr, ws, z1s, z1r, z2s, z2r, ags, agr, rss, rsr,
):
    c, h, g = lax.axis_index("ctx"), lax.axis_index("row"), lax.axis_index("col")

    def at(axis, index, by, n):
        return {axis: lax.rem(index + by, n)}

    def row(by):
        return at("row", h, by, ROWS)

    right, left = at("col", g, 1, 4), at("col", g, 3, 4)
    sends_tail = jnp.logical_and(h == ROWS - 1, c < CTX - 1)

    load_x = pltpu.make_async_copy(proj, x, ps)
    load_x.start()
    load_w = pltpu.make_async_copy(weight, w, ws)
    load_w.start()

    bar = pltpu.get_barrier_semaphore()

    def greet(where):
        pl.semaphore_signal(bar, inc=1, device_id=where, device_id_type=MESH)

    @pl.loop(1, CTX)
    def _(i):
        greet(at("ctx", c, i, CTX))

    @pl.when(jnp.logical_and(h != ROWS - 1, c > 0))
    def _():
        greet({"ctx": c - 1, "row": ROWS - 1})

    for i in range(1, ROWS):
        greet(row(i))
    greet(right)
    greet(left)

    lane = lax.broadcasted_iota(jnp.int32, (BLK, 128), 1)
    lane_q = lax.broadcasted_iota(jnp.int32, (BLK // 4, 128), 1)
    load_x.wait()
    for head in range(ROWS):
        y = pltpu.roll(
            x[:, head * DV : head * DV + WIN].astype(F32), WIN - 2 * FEAT * (head + 1), 1
        )
        for j in range(TILES):
            packed[head, j] = y[:, j * 128 : j * 128 + 128].astype(BF16)
        last = y[:, DV:]
        q = jnp.zeros((BLK // 4, 128), F32)
        for i in range(4):
            part_i = pltpu.roll(last[i * 64 : i * 64 + 64], 32 * (i + 1) % 128, 1)
            q = jnp.where(lane_q // 32 == i, part_i, q)
        quarter[head] = q.astype(BF16)
    window = taps[:, pl.ds(pl.multiple_of(h * DV, DV), WIN)]
    window = jnp.concatenate([window, jnp.zeros((5, WIN), F32)], axis=0)
    tap[...] = pltpu.roll(window, WIN - 2 * FEAT * (h + 1), 1)

    pl.semaphore_wait(bar, ROWS - 1 + CTX - 1 + 2 + jnp.where(sends_tail, ROWS - 1, 0))

    def spot(r):
        return pl.ds(pl.multiple_of(16 + r * BLK, 16), BLK)

    def send_values(i, j):
        return pltpu.make_async_remote_copy(
            packed.at[lax.rem(h + i, ROWS), j], raw.at[j, spot(h)], xs.at[i, j], xr.at[i, j], row(i), MESH
        )

    def send_keys(i):
        return pltpu.make_async_remote_copy(
            quarter.at[lax.rem(h + i, ROWS)], land.at[h], xs.at[i, 4], xr.at[i, 4], row(i), MESH
        )

    def tail(head):
        return pltpu.make_async_remote_copy(
            packed.at[head, :, pl.ds(BLK - 16, 16)],
            raw.at[:, pl.ds(0, 16)],
            ts.at[head],
            tr,
            {"ctx": lax.rem(c + 1, CTX), "row": head},
            MESH,
        )

    for i in (2, 1, 3):
        send_keys(i).start()

    @pl.when(sends_tail)
    def _():
        for head in range(ROWS):
            tail(head).start()

    for j in range(4):
        for i in (2, 1, 3):
            send_values(i, j).start()

    for j in range(4):
        raw[j, spot(h), :] = packed[h, j]
    land[h] = quarter[h]

    for i in (1, 3, 2):
        send_keys(i).wait_recv()
    for r in range(ROWS):
        q = land[r].astype(F32)
        for i in range(4):
            raw[4, 16 + r * BLK + i * 64 : 16 + r * BLK + i * 64 + 64, :] = pltpu.roll(
                q, 96 - 32 * i, 1
            ).astype(BF16)

    @pl.when(c == 0)
    def _():
        raw[:, 0:16, :] = jnp.zeros((TILES, 16, 128), BF16)

    @pl.when(c > 0)
    def _():
        tail(0).wait_recv()

    def gate(j, b, cols):
        v = raw[j, pl.ds(pl.multiple_of(b * BLK, 16), BLK + 16), :].astype(F32)
        t = [tap[i : i + 1, cols] for i in range(3)]
        return (v * (t[0] * v + t[1] * pltpu.roll(v, 1, 0) + t[2] * pltpu.roll(v, 2, 0)))[16:]

    ones = jnp.ones((8, BLK), BF16)
    k1, k2, q1, q2 = (select[i * FP : i * FP + FP] for i in range(4))
    move = select[4 * FP :]

    @pl.loop(0, ROWS)
    def _(b):
        qk = jnp.where(lane == 0, 1.0, gate(4, b, slice(DV, WIN))).astype(BF16)
        gated[pl.ds(pl.multiple_of(b * BLK, BLK), BLK), DV:] = qk
        phi = (dot_nt(k1, qk) * dot_nt(k2, qk)).astype(BF16)
        phik[b] = phi
        totals[b] = jnp.concatenate([dot_nt(ones, phi), jnp.zeros((8, DV - FP), F32)], axis=1)

    feature = lax.broadcasted_iota(jnp.int32, (FS, 128), 0)
    mine_rows = pl.ds(pl.multiple_of(lax.rem(c, 4) * SR, SR), SR)
    mine_cols = pl.ds(pl.multiple_of(lax.div(c, 4) * SC, SC), SC)

    def to_owner(o, source):
        return pltpu.make_async_remote_copy(
            mine.at[
                ROWS,
                pl.ds(pl.multiple_of(lax.rem(o, 4) * SR, SR), SR),
                pl.ds(pl.multiple_of(lax.div(o, 4) * SC, SC), SC),
            ],
            z1.at[source],
            z1s.at[o],
            z1r.at[source],
            {"ctx": o},
            MESH,
        )

    def from_owner(to, owner):
        return pltpu.make_async_remote_copy(
            z2.at[to], outer.at[mine_rows, mine_cols], z2s.at[to], z2r.at[owner], {"ctx": to}, MESH
        )

    def other(i):
        return lax.rem(c + i, CTX)

    def own_share():
        @pl.loop(1, CTX)
        def _(i):
            to_owner(c, other(i)).wait_recv()

        run = jnp.zeros((SR, SC), F32)
        for i in range(CTX):
            z2[i] = run.astype(BF16)
            run = run + z1[i].astype(F32)

        @pl.loop(1, CTX)
        def _(i):
            from_owner(other(i), c).start()

        outer[mine_rows, mine_cols] = z2[c]

    outer[FS:, :] = jnp.zeros((FP - FS, DV), BF16)

    @pl.loop(0, 4)
    def _(j):
        cols = pl.ds(pl.multiple_of(j * 128, 128), 128)
        for i in (1, 3, 2):
            send_values(i, j).wait_recv()
        inner[...] = jnp.zeros((FS, 128), F32)

        @pl.loop(0, ROWS)
        def _(b):
            value = gate(j, b, cols).astype(BF16)
            gated[pl.ds(pl.multiple_of(b * BLK, BLK), BLK), cols] = value
            state = jnp.where(
                feature == PHI, totals[b, 0:1, cols], dot(phik[b, :FS], value)
            )
            before = inner[...]
            mine[b, :, cols] = before.astype(BF16)
            inner[...] = before + state

        mine[ROWS, :, cols] = inner[...].astype(BF16)
        for i in range(4):
            o = j * 4 + i

            @pl.when(o != c)
            def _():
                to_owner(o, c).start()

            @pl.when(o == c)
            def _():
                z1[c] = mine[ROWS, mine_rows, mine_cols]

        @pl.when(lax.div(c, 4) == j - 1)
        def _():
            own_share()

    causal = lax.broadcasted_iota(jnp.int32, (BLK, BLK), 0) >= lax.broadcasted_iota(
        jnp.int32, (BLK, BLK), 1
    )

    @pl.loop(0, ROWS)
    def _(b):
        @pl.when(jnp.logical_and(b == 2, lax.div(c, 4) == 3))
        def _():
            own_share()

        rows = pl.ds(pl.multiple_of(b * BLK, BLK), BLK)
        qk = gated[rows, DV:]
        value = gated[rows, :DV]
        phi = (dot_nt(qk, q1) * dot_nt(qk, q2)).astype(BF16)
        phiq[rows, :] = phi
        z = dot_nt(dot_nt(qk, move).astype(BF16), qk)
        kern = jnp.where(causal, 1.0 + z + 0.5 * z * z, 0.0).astype(BF16)
        prior = mine[b]
        prior_total = prior[PHI : PHI + 1, :FP].astype(F32)
        num[rows, :] = dot(kern, value) + dot(phi[:, :FS], prior)
        weight_sum = jnp.sum(kern.astype(F32), axis=1, keepdims=True) + jnp.sum(
            phi.astype(F32) * prior_total, axis=1, keepdims=True
        )
        den[rows, :] = jnp.broadcast_to(weight_sum, (BLK, 128))

    @pl.loop(1, CTX)
    def _(i):
        from_owner(c, other(i)).wait_recv()

    load_w.wait()

    def head(by):
        return pl.ds(pl.multiple_of(lax.rem(h + by, ROWS) * DV, DV), DV)

    def ag(k, which):
        rows, of, to = (
            (pl.ds(0, CH), 0, 1),
            (pl.ds(0, CH), 0, 3),
            (pl.ds(0, CH // 2), 3, 1),
            (pl.ds(CH // 2, CH // 2), 1, 3),
        )[which]
        return pltpu.make_async_remote_copy(
            att.at[k, rows, head(of)],
            att.at[k, rows, head(of)],
            ags.at[k, which],
            agr.at[k, which],
            row(to),
            MESH,
        )

    def rs(k, which):
        a, b = pl.ds(0, HALF), pl.ds(HALF, HALF)
        j, cols, land, to = (
            (2, a, opp.at[k, 0], right),
            (2, b, opp.at[k, 1], left),
            (1, b, left_in.at[k, :, b], right),
            (3, a, right_in.at[k, :, a], left),
            (1, a, left_in.at[k, :, a], right),
            (3, b, right_in.at[k, :, b], left),
        )[which]
        return pltpu.make_async_remote_copy(
            part.at[k, pl.ds(j * T, T), cols], land, rss.at[k, which], rsr.at[k, which], to, MESH
        )

    outer_total = outer[PHI : PHI + 1, :FP].astype(F32)

    @pl.loop(0, K + 4)
    def _(step):
        @pl.when(step < K)
        def _():
            k = step
            places = [
                pl.ds(pl.multiple_of(lax.rem(g + j, ROWS) * BLK + k * T, T), T) for j in range(4)
            ]
            phi = jnp.concatenate([phiq[place, :] for place in places], axis=0)
            top = jnp.concatenate([num[place, :] for place in places], axis=0) + dot(phi, outer[...])
            bottom = jnp.concatenate([den[place, :] for place in places], axis=0)[:, 0:1] + jnp.sum(
                phi.astype(F32) * outer_total, axis=1, keepdims=True
            )
            att[k, :, head(0)] = (top / bottom).astype(BF16)
            ag(k, 0).start()
            ag(k, 1).start()

        @pl.when(jnp.logical_and(step >= 1, step < K + 1))
        def _():
            k = step - 1
            ag(k, 0).wait_recv()
            ag(k, 2).start()
            ag(k, 1).wait_recv()
            ag(k, 3).start()

        @pl.when(jnp.logical_and(step >= 2, step < K + 2))
        def _():
            k = step - 2
            ag(k, 2).wait_recv()
            ag(k, 3).wait_recv()
            for half in range(2):
                for n in range(2):
                    cols = slice(half * HALF + n * 512, half * HALF + n * 512 + 512)
                    p = dot(att[k], w[:, cols])
                    own[k, :, cols] = p[:T]
                    part[k, T:, cols] = p[T:].astype(BF16)
                for which in ((0, 3), (1, 2))[half]:
                    rs(k, which).start()

        @pl.when(jnp.logical_and(step >= 3, step < K + 3))
        def _():
            k = step - 3
            rs(k, 0).wait_recv()
            part[k, T : 2 * T, :HALF] = (
                part[k, T : 2 * T, :HALF].astype(F32) + opp[k, 0].astype(F32)
            ).astype(BF16)
            rs(k, 4).start()
            rs(k, 1).wait_recv()
            part[k, 3 * T :, HALF:] = (
                part[k, 3 * T :, HALF:].astype(F32) + opp[k, 1].astype(F32)
            ).astype(BF16)
            rs(k, 5).start()

        @pl.when(step >= 4)
        def _():
            k = step - 4
            for which in range(2, 6):
                rs(k, which).wait_recv()
            out[pl.ds(pl.multiple_of(k * T, T), T), :] = (
                own[k] + left_in[k].astype(F32) + right_in[k].astype(F32)
            ).astype(BF16)

    for i in (1, 2, 3):
        send_keys(i).wait_send()
        for j in range(4):
            send_values(i, j).wait_send()

    @pl.when(sends_tail)
    def _():
        for one in range(ROWS):
            tail(one).wait_send()

    @pl.loop(1, CTX)
    def _(i):
        to_owner(other(i), c).wait_send()
        from_owner(other(i), c).wait_send()

    @pl.loop(0, K)
    def _(k):
        for which in range(4):
            ag(k, which).wait_send()
        for which in range(6):
            rs(k, which).wait_send()


def shards(projected, conv_taps, out_weight):
    select = jnp.asarray(selectors(), BF16)
    vmem = pl.BlockSpec(memory_space=pltpu.VMEM)
    hbm = pl.BlockSpec(memory_space=pl.ANY)
    dma = pltpu.SemaphoreType.DMA
    return pl.pallas_call(
        kernel,
        out_shape=jax.ShapeDtypeStruct((BLK, 2048), BF16),
        in_specs=[hbm, vmem, hbm, vmem],
        out_specs=vmem,
        scratch_shapes=[
            pltpu.VMEM((BLK, ROWS * (2 * FEAT + DV)), BF16),
            pltpu.VMEM((ROWS, TILES, BLK, 128), BF16),
            pltpu.VMEM((ROWS, BLK // 4, 128), BF16),
            pltpu.VMEM((TILES, 16 + TOK, 128), BF16),
            pltpu.VMEM((ROWS, BLK // 4, 128), BF16),
            pltpu.VMEM((8, WIN), F32),
            pltpu.VMEM((TOK, WIN), BF16),
            pltpu.VMEM((ROWS, FP, BLK), BF16),
            pltpu.VMEM((ROWS, 8, DV), F32),
            pltpu.VMEM((TOK, DV), F32),
            pltpu.VMEM((TOK, 128), F32),
            pltpu.VMEM((TOK, FP), BF16),
            pltpu.VMEM((FS, 128), F32),
            pltpu.VMEM((ROWS + 1, FS, DV), BF16),
            pltpu.VMEM((CTX, SR, SC), BF16),
            pltpu.VMEM((CTX, SR, SC), BF16),
            pltpu.VMEM((FP, DV), BF16),
            pltpu.VMEM((2048, 2048), BF16),
            pltpu.VMEM((K, CH, 2048), BF16),
            pltpu.VMEM((K, CH, 2048), BF16),
            pltpu.VMEM((K, T, 2048), F32),
            pltpu.VMEM((K, 2, T, HALF), BF16),
            pltpu.VMEM((K, T, 2048), BF16),
            pltpu.VMEM((K, T, 2048), BF16),
            dma,
            dma((4, TILES)),
            dma((4, TILES)),
            dma((4,)),
            dma,
            dma,
            dma((CTX,)),
            dma((CTX,)),
            dma((CTX,)),
            dma((CTX,)),
            dma((K, 4)),
            dma((K, 4)),
            dma((K, 6)),
            dma((K, 6)),
        ],
        compiler_params=pltpu.CompilerParams(
            collective_id=0, has_side_effects=True, vmem_limit_bytes=56 * 2**20
        ),
    )(projected, conv_taps, out_weight, select)


def solution(mesh):
    in_specs = (P(("ctx", "row"), "col"), P(None, "col"), P("col", "row"))
    out_specs = P(("ctx", "col"), "row")
    return jax.shard_map(shards, mesh=mesh, in_specs=in_specs, out_specs=out_specs, check_vma=False)
```

```python
import jax
import jax.numpy as jnp
import numpy as np
from jax import lax
from jax.experimental import pallas as pl
from jax.experimental.pallas import tpu as pltpu
from jax.sharding import PartitionSpec as P

MESH = pl.DeviceIdType.MESH
FEAT = 16
DV = 512
PHI = 153
WIN = 640
BLK = 256
ROWS = 4
CTX = 16
TOK = ROWS * BLK
FP = 256
FS = 192
SR, SC = 48, 128
TILES = 5
K = 8
T, EDGE = 32, 32
HALF = 1024
Q0, K0 = 96, 112
F32, BF16 = jnp.float32, jnp.bfloat16
NT = (((1,), (1,)), ((), ()))


def selectors():
    first, second = np.triu_indices(FEAT)
    k1, k2, q1, q2 = (np.zeros((FP, 128), np.float32) for _ in range(4))
    for m in (k1, k2, q1, q2):
        m[0, 0] = 1.0
    for i in range(FEAT):
        k1[1 + i, K0 + i] = 1.0
        k2[1 + i, 0] = 1.0
        q1[1 + i, Q0 + i] = 1.0
        q2[1 + i, 0] = 0.25
    for n, (i, j) in enumerate(zip(first, second)):
        at = 1 + FEAT + n
        k1[at, K0 + i] = 1.0
        k2[at, K0 + j] = 1.0
        q1[at, Q0 + i] = 1.0
        q2[at, Q0 + j] = 1.0 / 32 if i == j else 1.0 / 16
    move = np.zeros((128, 128), np.float32)
    for i in range(FEAT):
        move[K0 + i, Q0 + i] = 0.25
    return np.concatenate([k1, k2, q1, q2, move])


def dot(a, b):
    return jnp.dot(a, b, preferred_element_type=F32)


def dot_nt(a, b):
    return lax.dot_general(a, b, NT, preferred_element_type=F32)


def kernel(
    proj, taps, weight, select, out,
    x, packed, quarter, raw, land, tap, gated, phik, totals, num, den, phiq,
    inner, mine, z1, z2, outer, w, att, part, own, opp, left_in, right_in,
    ps, xs, xr, ts, tr, ws, z1s, z1r, z2s, z2r, ags, agr, rss, rsr,
):
    c, h, g = lax.axis_index("ctx"), lax.axis_index("row"), lax.axis_index("col")

    def at(axis, index, by, n):
        return {axis: lax.rem(index + by, n)}

    def row(by):
        return at("row", h, by, ROWS)

    right, left = at("col", g, 1, 4), at("col", g, 3, 4)
    sends_tail = jnp.logical_and(h == ROWS - 1, c < CTX - 1)

    load_x = pltpu.make_async_copy(proj, x, ps)
    load_x.start()
    load_w = pltpu.make_async_copy(weight, w, ws)
    load_w.start()

    bar = pltpu.get_barrier_semaphore()

    def greet(where):
        pl.semaphore_signal(bar, inc=1, device_id=where, device_id_type=MESH)

    @pl.loop(1, CTX)
    def _(i):
        greet(at("ctx", c, i, CTX))

    @pl.when(jnp.logical_and(h != ROWS - 1, c > 0))
    def _():
        greet({"ctx": c - 1, "row": ROWS - 1})

    for i in range(1, ROWS):
        greet(row(i))
    greet(right)
    greet(left)

    lane = lax.broadcasted_iota(jnp.int32, (BLK, 128), 1)
    lane_q = lax.broadcasted_iota(jnp.int32, (BLK // 4, 128), 1)
    load_x.wait()
    for head in range(ROWS):
        y = pltpu.roll(
            x[:, head * DV : head * DV + WIN].astype(F32), WIN - 2 * FEAT * (head + 1), 1
        )
        for j in range(TILES):
            packed[head, j] = y[:, j * 128 : j * 128 + 128].astype(BF16)
        last = y[:, DV:]
        q = jnp.zeros((BLK // 4, 128), F32)
        for i in range(4):
            part_i = pltpu.roll(last[i * 64 : i * 64 + 64], 32 * (i + 1) % 128, 1)
            q = jnp.where(lane_q // 32 == i, part_i, q)
        quarter[head] = q.astype(BF16)
    window = taps[:, pl.ds(pl.multiple_of(h * DV, DV), WIN)]
    window = jnp.concatenate([window, jnp.zeros((5, WIN), F32)], axis=0)
    tap[...] = pltpu.roll(window, WIN - 2 * FEAT * (h + 1), 1)

    pl.semaphore_wait(bar, ROWS - 1 + CTX - 1 + 2 + jnp.where(sends_tail, ROWS - 1, 0))

    def spot(r):
        return pl.ds(pl.multiple_of(16 + r * BLK, 16), BLK)

    def send_values(i, j):
        return pltpu.make_async_remote_copy(
            packed.at[lax.rem(h + i, ROWS), j], raw.at[j, spot(h)], xs.at[i, j], xr.at[i, j], row(i), MESH
        )

    def send_keys(i):
        return pltpu.make_async_remote_copy(
            quarter.at[lax.rem(h + i, ROWS)], land.at[h], xs.at[i, 4], xr.at[i, 4], row(i), MESH
        )

    def tail(head):
        return pltpu.make_async_remote_copy(
            packed.at[head, :, pl.ds(BLK - 16, 16)],
            raw.at[:, pl.ds(0, 16)],
            ts.at[head],
            tr,
            {"ctx": lax.rem(c + 1, CTX), "row": head},
            MESH,
        )

    for i in (2, 1, 3):
        send_keys(i).start()

    @pl.when(sends_tail)
    def _():
        for head in range(ROWS):
            tail(head).start()

    for j in range(4):
        for i in (2, 1, 3):
            send_values(i, j).start()

    for j in range(4):
        raw[j, spot(h), :] = packed[h, j]
    land[h] = quarter[h]

    for i in (1, 3, 2):
        send_keys(i).wait_recv()
    for r in range(ROWS):
        q = land[r].astype(F32)
        for i in range(4):
            raw[4, 16 + r * BLK + i * 64 : 16 + r * BLK + i * 64 + 64, :] = pltpu.roll(
                q, 96 - 32 * i, 1
            ).astype(BF16)

    @pl.when(c == 0)
    def _():
        raw[:, 0:16, :] = jnp.zeros((TILES, 16, 128), BF16)

    @pl.when(c > 0)
    def _():
        tail(0).wait_recv()

    def gate(j, b, cols):
        v = raw[j, pl.ds(pl.multiple_of(b * BLK, 16), BLK + 16), :].astype(F32)
        t = [tap[i : i + 1, cols] for i in range(3)]
        return (v * (t[0] * v + t[1] * pltpu.roll(v, 1, 0) + t[2] * pltpu.roll(v, 2, 0)))[16:]

    ones = jnp.ones((8, BLK), BF16)
    k1, k2, q1, q2 = (select[i * FP : i * FP + FP] for i in range(4))
    move = select[4 * FP :]

    @pl.loop(0, ROWS)
    def _(b):
        qk = jnp.where(lane == 0, 1.0, gate(4, b, slice(DV, WIN))).astype(BF16)
        gated[pl.ds(pl.multiple_of(b * BLK, BLK), BLK), DV:] = qk
        phi = (dot_nt(k1, qk) * dot_nt(k2, qk)).astype(BF16)
        phik[b] = phi
        totals[b] = jnp.concatenate([dot_nt(ones, phi), jnp.zeros((8, DV - FP), F32)], axis=1)

    feature = lax.broadcasted_iota(jnp.int32, (FS, 128), 0)

    def share(o):
        tile, part_of = lax.rem(lax.div(o, 2), 4), 2 * lax.div(o, 8) + lax.rem(o, 2)
        return (
            pl.ds(pl.multiple_of(part_of * SR, SR), SR),
            pl.ds(pl.multiple_of(tile * SC, SC), SC),
        )

    mine_rows, mine_cols = share(c)

    def to_owner(o, source):
        rows, cols = share(o)
        return pltpu.make_async_remote_copy(
            mine.at[ROWS, rows, cols],
            z1.at[source],
            z1s.at[o],
            z1r.at[source],
            {"ctx": o},
            MESH,
        )

    def from_owner(to, owner):
        return pltpu.make_async_remote_copy(
            z2.at[to], outer.at[mine_rows, mine_cols], z2s.at[to], z2r.at[owner], {"ctx": to}, MESH
        )

    def other(i):
        return lax.rem(c + i, CTX)

    outer[FS:, :] = jnp.zeros((FP - FS, DV), BF16)

    @pl.loop(0, 4)
    def _(j):
        cols = pl.ds(pl.multiple_of(j * 128, 128), 128)
        for i in (1, 3, 2):
            send_values(i, j).wait_recv()
        inner[...] = jnp.zeros((FS, 128), F32)

        @pl.loop(0, ROWS)
        def _(b):
            value = gate(j, b, cols).astype(BF16)
            gated[pl.ds(pl.multiple_of(b * BLK, BLK), BLK), cols] = value
            state = jnp.where(
                feature == PHI, totals[b, 0:1, cols], dot(phik[b, :FS], value)
            )
            before = inner[...]
            mine[b, :, cols] = before.astype(BF16)
            inner[...] = before + state

        mine[ROWS, :, cols] = inner[...].astype(BF16)
        for i in range(4):
            o = 2 * j + 8 * (i // 2) + i % 2

            @pl.when(o != c)
            def _():
                to_owner(o, c).start()

            @pl.when(o == c)
            def _():
                z1[c] = mine[ROWS, mine_rows, mine_cols]

    causal = lax.broadcasted_iota(jnp.int32, (BLK, BLK), 0) >= lax.broadcasted_iota(
        jnp.int32, (BLK, BLK), 1
    )

    @pl.loop(0, ROWS)
    def _(b):
        rows = pl.ds(pl.multiple_of(b * BLK, BLK), BLK)
        qk = gated[rows, DV:]
        value = gated[rows, :DV]
        phi = (dot_nt(qk, q1) * dot_nt(qk, q2)).astype(BF16)
        phiq[rows, :] = phi
        z = dot_nt(dot_nt(qk, move).astype(BF16), qk)
        kern = jnp.where(causal, 1.0 + z + 0.5 * z * z, 0.0).astype(BF16)
        prior = mine[b]
        prior_total = prior[PHI : PHI + 1, :FP].astype(F32)
        num[rows, :] = dot(kern, value) + dot(phi[:, :FS], prior)
        weight_sum = jnp.sum(kern.astype(F32), axis=1, keepdims=True) + jnp.sum(
            phi.astype(F32) * prior_total, axis=1, keepdims=True
        )
        den[rows, :] = jnp.broadcast_to(weight_sum, (BLK, 128))

    @pl.loop(1, CTX)
    def _(i):
        to_owner(c, other(i)).wait_recv()

    run = jnp.zeros((SR, SC), F32)
    for i in range(CTX):
        z2[i] = run.astype(BF16)
        run = run + z1[i].astype(F32)

    @pl.loop(1, CTX)
    def _(i):
        from_owner(other(i), c).start()

    outer[mine_rows, mine_cols] = z2[c]

    @pl.loop(1, CTX)
    def _(i):
        from_owner(c, other(i)).wait_recv()

    load_w.wait()

    def head(by):
        return pl.ds(pl.multiple_of(lax.rem(h + by, ROWS) * DV, DV), DV)

    def begin(k):
        return jnp.where(k == K - 1, BLK - EDGE, jnp.maximum(k * T - (T - EDGE), 0))

    def tokens(k, n):
        return pl.ds(pl.multiple_of(begin(k), EDGE), n)

    def chunk(k, first, n):
        return pl.ds(pl.multiple_of(begin(k) * 4 + first, EDGE), n)

    def ag(k, n, which):
        first, size, of, to = ((0, 4 * n, 0, 1), (0, 4 * n, 0, 3), (0, 2 * n, 3, 1), (2 * n, 2 * n, 1, 3))[which]
        ref = att.at[chunk(k, first, size), head(of)]
        return pltpu.make_async_remote_copy(ref, ref, ags.at[k, which], agr.at[k, which], row(to), MESH)

    def rs(k, n, which):
        a, b, t = pl.ds(0, HALF), pl.ds(HALF, HALF), tokens(k, n)
        j, cols, to_ref, to = (
            (2, a, opp.at[0, t], right),
            (2, b, opp.at[1, t], left),
            (1, b, left_in.at[t, b], right),
            (3, a, right_in.at[t, a], left),
            (1, a, left_in.at[t, a], right),
            (3, b, right_in.at[t, b], left),
        )[which]
        return pltpu.make_async_remote_copy(
            part.at[chunk(k, j * n, n), cols], to_ref, rss.at[k, which], rsr.at[k, which], to, MESH
        )

    outer_total = outer[PHI : PHI + 1, :FP].astype(F32)

    def attend(k, n):
        places = [
            pl.ds(pl.multiple_of(lax.rem(g + j, ROWS) * BLK + begin(k), EDGE), n) for j in range(4)
        ]
        phi = jnp.concatenate([phiq[place, :] for place in places], axis=0)
        top = jnp.concatenate([num[place, :] for place in places], axis=0) + dot(phi, outer[...])
        bottom = jnp.concatenate([den[place, :] for place in places], axis=0)[:, 0:1] + jnp.sum(
            phi.astype(F32) * outer_total, axis=1, keepdims=True
        )
        att[chunk(k, 0, 4 * n), head(0)] = (top / bottom).astype(BF16)
        ag(k, n, 0).start()
        ag(k, n, 1).start()

    def forward(k, n):
        ag(k, n, 0).wait_recv()
        ag(k, n, 2).start()
        ag(k, n, 1).wait_recv()
        ag(k, n, 3).start()

    def project(k, n):
        ag(k, n, 2).wait_recv()
        ag(k, n, 3).wait_recv()
        for half in range(2):
            for m in range(2):
                cols = slice(half * HALF + m * 512, half * HALF + m * 512 + 512)
                p = dot(att[chunk(k, 0, 4 * n), :], w[:, cols])
                own[tokens(k, n), cols] = p[:n]
                part[chunk(k, n, 3 * n), cols] = p[n:].astype(BF16)
            for which in ((0, 3), (1, 2))[half]:
                rs(k, n, which).start()

    def join(k, n):
        for side, j, cols in ((0, 1, slice(0, HALF)), (1, 3, slice(HALF, 2 * HALF))):
            rs(k, n, side).wait_recv()
            rows = chunk(k, j * n, n)
            both = part[rows, cols].astype(F32) + opp[side, tokens(k, n), :].astype(F32)
            part[rows, cols] = both.astype(BF16)
            rs(k, n, 4 + side).start()

    def finish(k, n):
        for which in range(2, 6):
            rs(k, n, which).wait_recv()
        t = tokens(k, n)
        out[t, :] = (own[t, :] + left_in[t, :].astype(F32) + right_in[t, :].astype(F32)).astype(BF16)

    def sized(k, stage):
        edge = jnp.logical_or(k == 0, k == K - 1)

        @pl.when(edge)
        def _():
            stage(k, EDGE)

        @pl.when(jnp.logical_not(edge))
        def _():
            stage(k, T)

    @pl.loop(0, K + 4)
    def _(step):
        for late, stage in enumerate((attend, forward, project, join, finish)):

            @pl.when(jnp.logical_and(step >= late, step < K + late))
            def _():
                sized(step - late, stage)

    for i in (1, 2, 3):
        send_keys(i).wait_send()
        for j in range(4):
            send_values(i, j).wait_send()

    @pl.when(sends_tail)
    def _():
        for one in range(ROWS):
            tail(one).wait_send()

    @pl.loop(1, CTX)
    def _(i):
        to_owner(other(i), c).wait_send()
        from_owner(other(i), c).wait_send()

    def sent(k, n):
        for which in range(4):
            ag(k, n, which).wait_send()
        for which in range(6):
            rs(k, n, which).wait_send()

    @pl.loop(0, K)
    def _(k):
        sized(k, sent)


def shards(projected, conv_taps, out_weight):
    select = jnp.asarray(selectors(), BF16)
    vmem = pl.BlockSpec(memory_space=pltpu.VMEM)
    hbm = pl.BlockSpec(memory_space=pl.ANY)
    dma = pltpu.SemaphoreType.DMA
    return pl.pallas_call(
        kernel,
        out_shape=jax.ShapeDtypeStruct((BLK, 2048), BF16),
        in_specs=[hbm, vmem, hbm, vmem],
        out_specs=vmem,
        scratch_shapes=[
            pltpu.VMEM((BLK, ROWS * (2 * FEAT + DV)), BF16),
            pltpu.VMEM((ROWS, TILES, BLK, 128), BF16),
            pltpu.VMEM((ROWS, BLK // 4, 128), BF16),
            pltpu.VMEM((TILES, 16 + TOK, 128), BF16),
            pltpu.VMEM((ROWS, BLK // 4, 128), BF16),
            pltpu.VMEM((8, WIN), F32),
            pltpu.VMEM((TOK, WIN), BF16),
            pltpu.VMEM((ROWS, FP, BLK), BF16),
            pltpu.VMEM((ROWS, 8, DV), F32),
            pltpu.VMEM((TOK, DV), F32),
            pltpu.VMEM((TOK, 128), F32),
            pltpu.VMEM((TOK, FP), BF16),
            pltpu.VMEM((FS, 128), F32),
            pltpu.VMEM((ROWS + 1, FS, DV), BF16),
            pltpu.VMEM((CTX, SR, SC), BF16),
            pltpu.VMEM((CTX, SR, SC), BF16),
            pltpu.VMEM((FP, DV), BF16),
            pltpu.VMEM((2048, 2048), BF16),
            pltpu.VMEM((TOK, 2048), BF16),
            pltpu.VMEM((TOK, 2048), BF16),
            pltpu.VMEM((BLK, 2048), F32),
            pltpu.VMEM((2, BLK, HALF), BF16),
            pltpu.VMEM((BLK, 2048), BF16),
            pltpu.VMEM((BLK, 2048), BF16),
            dma,
            dma((4, TILES)),
            dma((4, TILES)),
            dma((4,)),
            dma,
            dma,
            dma((CTX,)),
            dma((CTX,)),
            dma((CTX,)),
            dma((CTX,)),
            dma((K, 4)),
            dma((K, 4)),
            dma((K, 6)),
            dma((K, 6)),
        ],
        compiler_params=pltpu.CompilerParams(
            collective_id=0, has_side_effects=True, vmem_limit_bytes=56 * 2**20
        ),
    )(projected, conv_taps, out_weight, select)


def solution(mesh):
    in_specs = (P(("ctx", "row"), "col"), P(None, "col"), P("col", "row"))
    out_specs = P(("ctx", "col"), "row")
    return jax.shard_map(shards, mesh=mesh, in_specs=in_specs, out_specs=out_specs, check_vma=False)
```

```python
import jax
import jax.numpy as jnp
import numpy as np
from jax import lax
from jax.experimental import pallas as pl
from jax.experimental.pallas import tpu as pltpu
from jax.sharding import PartitionSpec as P

MESH = pl.DeviceIdType.MESH
FEAT = 16
DV = 512
PHI = 153
WIN = 640
BLK = 256
ROWS = 4
CTX = 16
TOK = ROWS * BLK
FP = 256
FS = 192
SR, SC = 48, 128
TILES = 5
K = 8
T, EDGE = 32, 32
HALF = 1024
Q0, K0 = 96, 112
F32, BF16 = jnp.float32, jnp.bfloat16
NT = (((1,), (1,)), ((), ()))


def selectors():
    first, second = np.triu_indices(FEAT)
    k1, k2, q1, q2 = (np.zeros((FP, 128), np.float32) for _ in range(4))
    for m in (k1, k2, q1, q2):
        m[0, 0] = 1.0
    for i in range(FEAT):
        k1[1 + i, K0 + i] = 1.0
        k2[1 + i, 0] = 1.0
        q1[1 + i, Q0 + i] = 1.0
        q2[1 + i, 0] = 0.25
    for n, (i, j) in enumerate(zip(first, second)):
        at = 1 + FEAT + n
        k1[at, K0 + i] = 1.0
        k2[at, K0 + j] = 1.0
        q1[at, Q0 + i] = 1.0
        q2[at, Q0 + j] = 1.0 / 32 if i == j else 1.0 / 16
    move = np.zeros((128, 128), np.float32)
    for i in range(FEAT):
        move[K0 + i, Q0 + i] = 0.25
    return np.concatenate([k1, k2, q1, q2, move])


def dot(a, b):
    return jnp.dot(a, b, preferred_element_type=F32)


def dot_nt(a, b):
    return lax.dot_general(a, b, NT, preferred_element_type=F32)


def kernel(
    proj, taps, weight, select, out,
    x, packed, quarter, raw, land, tap, gated, phik, totals, num, den, phiq,
    inner, mine, z1, z2, outer, w, att, part, own, opp, left_in, right_in,
    ps, xs, xr, ts, tr, ws, z1s, z1r, z2s, z2r, ags, agr, rss, rsr,
):
    c, h, g = lax.axis_index("ctx"), lax.axis_index("row"), lax.axis_index("col")

    def at(axis, index, by, n):
        return {axis: lax.rem(index + by, n)}

    def row(by):
        return at("row", h, by, ROWS)

    right, left = at("col", g, 1, 4), at("col", g, 3, 4)
    sends_tail = jnp.logical_and(h == ROWS - 1, c < CTX - 1)

    load_x = pltpu.make_async_copy(proj, x, ps)
    load_x.start()
    load_w = pltpu.make_async_copy(weight, w, ws)
    load_w.start()

    bar = pltpu.get_barrier_semaphore()

    def greet(where):
        pl.semaphore_signal(bar, inc=1, device_id=where, device_id_type=MESH)

    @pl.loop(1, CTX)
    def _(i):
        greet(at("ctx", c, i, CTX))

    @pl.when(jnp.logical_and(h != ROWS - 1, c > 0))
    def _():
        greet({"ctx": c - 1, "row": ROWS - 1})

    for i in range(1, ROWS):
        greet(row(i))
    greet(right)
    greet(left)

    lane = lax.broadcasted_iota(jnp.int32, (BLK, 128), 1)
    lane_q = lax.broadcasted_iota(jnp.int32, (BLK // 4, 128), 1)
    load_x.wait()
    for head in range(ROWS):
        y = pltpu.roll(
            x[:, head * DV : head * DV + WIN].astype(F32), WIN - 2 * FEAT * (head + 1), 1
        )
        for j in range(TILES):
            packed[head, j] = y[:, j * 128 : j * 128 + 128].astype(BF16)
        last = y[:, DV:]
        q = jnp.zeros((BLK // 4, 128), F32)
        for i in range(4):
            part_i = pltpu.roll(last[i * 64 : i * 64 + 64], 32 * (i + 1) % 128, 1)
            q = jnp.where(lane_q // 32 == i, part_i, q)
        quarter[head] = q.astype(BF16)
    window = taps[:, pl.ds(pl.multiple_of(h * DV, DV), WIN)]
    window = jnp.concatenate([window, jnp.zeros((5, WIN), F32)], axis=0)
    tap[...] = pltpu.roll(window, WIN - 2 * FEAT * (h + 1), 1)

    pl.semaphore_wait(bar, ROWS - 1 + CTX - 1 + 2 + jnp.where(sends_tail, ROWS - 1, 0))

    def spot(r):
        return pl.ds(pl.multiple_of(16 + r * BLK, 16), BLK)

    def send_values(i, j):
        return pltpu.make_async_remote_copy(
            packed.at[lax.rem(h + i, ROWS), j], raw.at[j, spot(h)], xs.at[i, j], xr.at[i, j], row(i), MESH
        )

    def send_keys(i):
        return pltpu.make_async_remote_copy(
            quarter.at[lax.rem(h + i, ROWS)], land.at[h], xs.at[i, 4], xr.at[i, 4], row(i), MESH
        )

    def tail(head):
        return pltpu.make_async_remote_copy(
            packed.at[head, :, pl.ds(BLK - 16, 16)],
            raw.at[:, pl.ds(0, 16)],
            ts.at[head],
            tr,
            {"ctx": lax.rem(c + 1, CTX), "row": head},
            MESH,
        )

    for i in (2, 1, 3):
        send_keys(i).start()

    @pl.when(sends_tail)
    def _():
        for head in range(ROWS):
            tail(head).start()

    for j in range(4):
        for i in (2, 1, 3):
            send_values(i, j).start()

    for j in range(4):
        raw[j, spot(h), :] = packed[h, j]
    land[h] = quarter[h]

    for i in (1, 3, 2):
        send_keys(i).wait_recv()
    for r in range(ROWS):
        q = land[r].astype(F32)
        for i in range(4):
            raw[4, 16 + r * BLK + i * 64 : 16 + r * BLK + i * 64 + 64, :] = pltpu.roll(
                q, 96 - 32 * i, 1
            ).astype(BF16)

    @pl.when(c == 0)
    def _():
        raw[:, 0:16, :] = jnp.zeros((TILES, 16, 128), BF16)

    @pl.when(c > 0)
    def _():
        tail(0).wait_recv()

    def gate(j, b, cols):
        v = raw[j, pl.ds(pl.multiple_of(b * BLK, 16), BLK + 16), :].astype(F32)
        t = [tap[i : i + 1, cols] for i in range(3)]
        return (v * (t[0] * v + t[1] * pltpu.roll(v, 1, 0) + t[2] * pltpu.roll(v, 2, 0)))[16:]

    ones = jnp.ones((8, BLK), BF16)
    k1, k2, q1, q2 = (select[i * FP : i * FP + FP] for i in range(4))
    move = select[4 * FP :]

    @pl.loop(0, ROWS)
    def _(b):
        qk = jnp.where(lane == 0, 1.0, gate(4, b, slice(DV, WIN))).astype(BF16)
        gated[pl.ds(pl.multiple_of(b * BLK, BLK), BLK), DV:] = qk
        phi = (dot_nt(k1, qk) * dot_nt(k2, qk)).astype(BF16)
        phik[b] = phi
        totals[b] = jnp.concatenate([dot_nt(ones, phi), jnp.zeros((8, DV - FP), F32)], axis=1)

    feature = lax.broadcasted_iota(jnp.int32, (FS, 128), 0)

    def share(o):
        tile, part_of = lax.rem(lax.div(o, 2), 4), 2 * lax.div(o, 8) + lax.rem(o, 2)
        return (
            pl.ds(pl.multiple_of(part_of * SR, SR), SR),
            pl.ds(pl.multiple_of(tile * SC, SC), SC),
        )

    mine_rows, mine_cols = share(c)

    def to_owner(o, source):
        rows, cols = share(o)
        return pltpu.make_async_remote_copy(
            mine.at[ROWS, rows, cols],
            z1.at[source],
            z1s.at[o],
            z1r.at[source],
            {"ctx": o},
            MESH,
        )

    def from_owner(to, owner):
        return pltpu.make_async_remote_copy(
            z2.at[to], outer.at[mine_rows, mine_cols], z2s.at[to], z2r.at[owner], {"ctx": to}, MESH
        )

    def other(i):
        return lax.rem(c + i, CTX)

    outer[FS:, :] = jnp.zeros((FP - FS, DV), BF16)

    @pl.loop(0, 4)
    def _(j):
        cols = pl.ds(pl.multiple_of(j * 128, 128), 128)
        for i in (1, 3, 2):
            send_values(i, j).wait_recv()
        inner[...] = jnp.zeros((FS, 128), F32)

        @pl.loop(0, ROWS)
        def _(b):
            value = gate(j, b, cols).astype(BF16)
            gated[pl.ds(pl.multiple_of(b * BLK, BLK), BLK), cols] = value
            state = jnp.where(
                feature == PHI, totals[b, 0:1, cols], dot(phik[b, :FS], value)
            )
            before = inner[...]
            mine[b, :, cols] = before.astype(BF16)
            inner[...] = before + state

        mine[ROWS, :, cols] = inner[...].astype(BF16)
        for i in range(4):
            o = 2 * j + 8 * (i // 2) + i % 2

            @pl.when(o != c)
            def _():
                to_owner(o, c).start()

            @pl.when(o == c)
            def _():
                z1[c] = mine[ROWS, mine_rows, mine_cols]

    causal = lax.broadcasted_iota(jnp.int32, (BLK, BLK), 0) >= lax.broadcasted_iota(
        jnp.int32, (BLK, BLK), 1
    )

    @pl.loop(0, ROWS)
    def _(b):
        rows = pl.ds(pl.multiple_of(b * BLK, BLK), BLK)
        qk = gated[rows, DV:]
        value = gated[rows, :DV]
        phi = (dot_nt(qk, q1) * dot_nt(qk, q2)).astype(BF16)
        phiq[rows, :] = phi
        z = dot_nt(dot_nt(qk, move).astype(BF16), qk)
        kern = jnp.where(causal, 1.0 + z + 0.5 * z * z, 0.0).astype(BF16)
        prior = mine[b]
        prior_total = prior[PHI : PHI + 1, :FP].astype(F32)
        num[rows, :] = dot(kern, value) + dot(phi[:, :FS], prior)
        weight_sum = jnp.sum(kern.astype(F32), axis=1, keepdims=True) + jnp.sum(
            phi.astype(F32) * prior_total, axis=1, keepdims=True
        )
        den[rows, :] = jnp.broadcast_to(weight_sum, (BLK, 128))

    @pl.loop(1, CTX)
    def _(i):
        to_owner(c, other(i)).wait_recv()

    run = jnp.zeros((SR, SC), F32)
    for i in range(CTX):
        z2[i] = run.astype(BF16)
        run = run + z1[i].astype(F32)

    @pl.loop(1, CTX)
    def _(i):
        from_owner(other(i), c).start()

    outer[mine_rows, mine_cols] = z2[c]

    @pl.loop(1, CTX)
    def _(i):
        from_owner(c, other(i)).wait_recv()

    load_w.wait()

    def head(by):
        return pl.ds(pl.multiple_of(lax.rem(h + by, ROWS) * DV, DV), DV)

    def begin(k):
        return jnp.where(k == K - 1, BLK - EDGE, jnp.maximum(k * T - (T - EDGE), 0))

    def tokens(k, n):
        return pl.ds(pl.multiple_of(begin(k), EDGE), n)

    def chunk(k, first, n):
        return pl.ds(pl.multiple_of(begin(k) * 4 + first, EDGE), n)

    def ag(k, n, which):
        first, size, of, to = ((0, 4 * n, 0, 1), (0, 4 * n, 0, 3), (0, 2 * n, 3, 1), (2 * n, 2 * n, 1, 3))[which]
        ref = att.at[chunk(k, first, size), head(of)]
        return pltpu.make_async_remote_copy(ref, ref, ags.at[k, which], agr.at[k, which], row(to), MESH)

    def rs(k, n, which):
        a, b, t = pl.ds(0, HALF), pl.ds(HALF, HALF), tokens(k, n)
        j, cols, to_ref, to = (
            (2, a, opp.at[0, t], right),
            (2, b, opp.at[1, t], left),
            (1, b, left_in.at[t, b], right),
            (3, a, right_in.at[t, a], left),
            (1, a, left_in.at[t, a], right),
            (3, b, right_in.at[t, b], left),
        )[which]
        return pltpu.make_async_remote_copy(
            part.at[chunk(k, j * n, n), cols], to_ref, rss.at[k, which], rsr.at[k, which], to, MESH
        )

    outer_total = outer[PHI : PHI + 1, :FP].astype(F32)

    def attend(k, n):
        places = [
            pl.ds(pl.multiple_of(lax.rem(g + j, ROWS) * BLK + begin(k), EDGE), n) for j in range(4)
        ]
        phi = jnp.concatenate([phiq[place, :] for place in places], axis=0)
        top = jnp.concatenate([num[place, :] for place in places], axis=0) + dot(phi, outer[...])
        bottom = jnp.concatenate([den[place, :] for place in places], axis=0)[:, 0:1] + jnp.sum(
            phi.astype(F32) * outer_total, axis=1, keepdims=True
        )
        att[chunk(k, 0, 4 * n), head(0)] = (top / bottom).astype(BF16)
        ag(k, n, 0).start()
        ag(k, n, 1).start()

    def forward(k, n):
        ag(k, n, 0).wait_recv()
        ag(k, n, 2).start()
        ag(k, n, 1).wait_recv()
        ag(k, n, 3).start()

    def project(k, n):
        ag(k, n, 2).wait_recv()
        ag(k, n, 3).wait_recv()
        for half in range(2):
            for m in range(2):
                cols = slice(half * HALF + m * 512, half * HALF + m * 512 + 512)
                p = dot(att[chunk(k, 0, 4 * n), :], w[:, cols])
                own[tokens(k, n), cols] = p[:n]
                part[chunk(k, n, 3 * n), cols] = p[n:].astype(BF16)
            for which in ((0, 3), (1, 2))[half]:
                rs(k, n, which).start()

    def join(k, n):
        for side, j, cols in ((0, 1, slice(0, HALF)), (1, 3, slice(HALF, 2 * HALF))):
            rs(k, n, side).wait_recv()
            rows = chunk(k, j * n, n)
            both = part[rows, cols].astype(F32) + opp[side, tokens(k, n), :].astype(F32)
            part[rows, cols] = both.astype(BF16)
            rs(k, n, 4 + side).start()

    def finish(k, n):
        for which in range(2, 6):
            rs(k, n, which).wait_recv()
        t = tokens(k, n)
        out[t, :] = (own[t, :] + left_in[t, :].astype(F32) + right_in[t, :].astype(F32)).astype(BF16)

    def sized(k, stage):
        edge = jnp.logical_or(k == 0, k == K - 1)

        @pl.when(edge)
        def _():
            stage(k, EDGE)

        @pl.when(jnp.logical_not(edge))
        def _():
            stage(k, T)

    @pl.loop(0, K + 5)
    def _(step):
        for stage, late in ((attend, 0), (forward, 1), (project, 2), (join, 3), (finish, 5)):

            @pl.when(jnp.logical_and(step >= late, step < K + late))
            def _():
                sized(step - late, stage)

    for i in (1, 2, 3):
        send_keys(i).wait_send()
        for j in range(4):
            send_values(i, j).wait_send()

    @pl.when(sends_tail)
    def _():
        for one in range(ROWS):
            tail(one).wait_send()

    @pl.loop(1, CTX)
    def _(i):
        to_owner(other(i), c).wait_send()
        from_owner(other(i), c).wait_send()

    def sent(k, n):
        for which in range(4):
            ag(k, n, which).wait_send()
        for which in range(6):
            rs(k, n, which).wait_send()

    @pl.loop(0, K)
    def _(k):
        sized(k, sent)


def shards(projected, conv_taps, out_weight):
    select = jnp.asarray(selectors(), BF16)
    vmem = pl.BlockSpec(memory_space=pltpu.VMEM)
    hbm = pl.BlockSpec(memory_space=pl.ANY)
    dma = pltpu.SemaphoreType.DMA
    return pl.pallas_call(
        kernel,
        out_shape=jax.ShapeDtypeStruct((BLK, 2048), BF16),
        in_specs=[hbm, vmem, hbm, vmem],
        out_specs=vmem,
        scratch_shapes=[
            pltpu.VMEM((BLK, ROWS * (2 * FEAT + DV)), BF16),
            pltpu.VMEM((ROWS, TILES, BLK, 128), BF16),
            pltpu.VMEM((ROWS, BLK // 4, 128), BF16),
            pltpu.VMEM((TILES, 16 + TOK, 128), BF16),
            pltpu.VMEM((ROWS, BLK // 4, 128), BF16),
            pltpu.VMEM((8, WIN), F32),
            pltpu.VMEM((TOK, WIN), BF16),
            pltpu.VMEM((ROWS, FP, BLK), BF16),
            pltpu.VMEM((ROWS, 8, DV), F32),
            pltpu.VMEM((TOK, DV), F32),
            pltpu.VMEM((TOK, 128), F32),
            pltpu.VMEM((TOK, FP), BF16),
            pltpu.VMEM((FS, 128), F32),
            pltpu.VMEM((ROWS + 1, FS, DV), BF16),
            pltpu.VMEM((CTX, SR, SC), BF16),
            pltpu.VMEM((CTX, SR, SC), BF16),
            pltpu.VMEM((FP, DV), BF16),
            pltpu.VMEM((2048, 2048), BF16),
            pltpu.VMEM((TOK, 2048), BF16),
            pltpu.VMEM((TOK, 2048), BF16),
            pltpu.VMEM((BLK, 2048), F32),
            pltpu.VMEM((2, BLK, HALF), BF16),
            pltpu.VMEM((BLK, 2048), BF16),
            pltpu.VMEM((BLK, 2048), BF16),
            dma,
            dma((4, TILES)),
            dma((4, TILES)),
            dma((4,)),
            dma,
            dma,
            dma((CTX,)),
            dma((CTX,)),
            dma((CTX,)),
            dma((CTX,)),
            dma((K, 4)),
            dma((K, 4)),
            dma((K, 6)),
            dma((K, 6)),
        ],
        compiler_params=pltpu.CompilerParams(
            collective_id=0, has_side_effects=True, vmem_limit_bytes=56 * 2**20
        ),
    )(projected, conv_taps, out_weight, select)


def solution(mesh):
    in_specs = (P(("ctx", "row"), "col"), P(None, "col"), P("col", "row"))
    out_specs = P(("ctx", "col"), "row")
    return jax.shard_map(shards, mesh=mesh, in_specs=in_specs, out_specs=out_specs, check_vma=False)
```

```python
import jax
import jax.numpy as jnp
import numpy as np
from jax import lax
from jax.experimental import pallas as pl
from jax.experimental.pallas import tpu as pltpu
from jax.sharding import PartitionSpec as P

MESH = pl.DeviceIdType.MESH
FEAT = 16
DV = 512
PHI = 153
WIN = 640
BLK = 256
ROWS = 4
CTX = 16
TOK = ROWS * BLK
FP = 256
FS = 192
SR, SC = 48, 128
TILES = 5
K = 8
T, EDGE = 32, 32
HALF = 1024
Q0, K0 = 96, 112
F32, BF16 = jnp.float32, jnp.bfloat16
NT = (((1,), (1,)), ((), ()))


def selectors():
    first, second = np.triu_indices(FEAT)
    k1, k2, q1, q2 = (np.zeros((FP, 128), np.float32) for _ in range(4))
    for m in (k1, k2, q1, q2):
        m[0, 0] = 1.0
    for i in range(FEAT):
        k1[1 + i, K0 + i] = 1.0
        k2[1 + i, 0] = 1.0
        q1[1 + i, Q0 + i] = 1.0
        q2[1 + i, 0] = 0.25
    for n, (i, j) in enumerate(zip(first, second)):
        at = 1 + FEAT + n
        k1[at, K0 + i] = 1.0
        k2[at, K0 + j] = 1.0
        q1[at, Q0 + i] = 1.0
        q2[at, Q0 + j] = 1.0 / 32 if i == j else 1.0 / 16
    move = np.zeros((128, 128), np.float32)
    for i in range(FEAT):
        move[K0 + i, Q0 + i] = 0.25
    return np.concatenate([k1, k2, q1, q2, move])


def dot(a, b):
    return jnp.dot(a, b, preferred_element_type=F32)


def dot_nt(a, b):
    return lax.dot_general(a, b, NT, preferred_element_type=F32)


def kernel(
    proj, taps_in, weight, select_in, out_to,
    x, taps, select, out, packed, quarter, raw, land, tap, gated, phik, totals, num, den, phiq,
    inner, mine, z1, z2, outer, w, att, part, own, opp, left_in, right_in,
    ps, os, xs, xr, ts, tr, ws, z1s, z1r, z2s, z2r, ags, agr, rss, rsr,
):
    c, h, g = lax.axis_index("ctx"), lax.axis_index("row"), lax.axis_index("col")

    def at(axis, index, by, n):
        return {axis: lax.rem(index + by, n)}

    def row(by):
        return at("row", h, by, ROWS)

    right, left = at("col", g, 1, 4), at("col", g, 3, 4)
    sends_tail = jnp.logical_and(h == ROWS - 1, c < CTX - 1)

    load_x = pltpu.make_async_copy(proj, x, ps.at[0])
    load_x.start()
    load_taps = pltpu.make_async_copy(taps_in, taps, ps.at[1])
    load_taps.start()
    load_select = pltpu.make_async_copy(select_in, select, ps.at[2])
    load_select.start()
    load_w = pltpu.make_async_copy(weight, w, ws)
    load_w.start()

    bar = pltpu.get_barrier_semaphore()

    def greet(where):
        pl.semaphore_signal(bar, inc=1, device_id=where, device_id_type=MESH)

    @pl.loop(1, CTX)
    def _(i):
        greet(at("ctx", c, i, CTX))

    @pl.when(jnp.logical_and(h != ROWS - 1, c > 0))
    def _():
        greet({"ctx": c - 1, "row": ROWS - 1})

    for i in range(1, ROWS):
        greet(row(i))
    greet(right)
    greet(left)

    lane = lax.broadcasted_iota(jnp.int32, (BLK, 128), 1)
    lane_q = lax.broadcasted_iota(jnp.int32, (BLK // 4, 128), 1)
    load_x.wait()
    for head in range(ROWS):
        y = pltpu.roll(
            x[:, head * DV : head * DV + WIN].astype(F32), WIN - 2 * FEAT * (head + 1), 1
        )
        for j in range(TILES):
            packed[head, j] = y[:, j * 128 : j * 128 + 128].astype(BF16)
        last = y[:, DV:]
        q = jnp.zeros((BLK // 4, 128), F32)
        for i in range(4):
            part_i = pltpu.roll(last[i * 64 : i * 64 + 64], 32 * (i + 1) % 128, 1)
            q = jnp.where(lane_q // 32 == i, part_i, q)
        quarter[head] = q.astype(BF16)
    load_taps.wait()
    window = taps[:, pl.ds(pl.multiple_of(h * DV, DV), WIN)]
    window = jnp.concatenate([window, jnp.zeros((5, WIN), F32)], axis=0)
    tap[...] = pltpu.roll(window, WIN - 2 * FEAT * (h + 1), 1)

    pl.semaphore_wait(bar, ROWS - 1 + CTX - 1 + 2 + jnp.where(sends_tail, ROWS - 1, 0))

    def spot(r):
        return pl.ds(pl.multiple_of(16 + r * BLK, 16), BLK)

    def send_values(i, j):
        return pltpu.make_async_remote_copy(
            packed.at[lax.rem(h + i, ROWS), j], raw.at[j, spot(h)], xs.at[i, j], xr.at[i, j], row(i), MESH
        )

    def send_keys(i):
        return pltpu.make_async_remote_copy(
            quarter.at[lax.rem(h + i, ROWS)], land.at[h], xs.at[i, 4], xr.at[i, 4], row(i), MESH
        )

    def tail(head):
        return pltpu.make_async_remote_copy(
            packed.at[head, :, pl.ds(BLK - 16, 16)],
            raw.at[:, pl.ds(0, 16)],
            ts.at[head],
            tr,
            {"ctx": lax.rem(c + 1, CTX), "row": head},
            MESH,
        )

    for i in (2, 1, 3):
        send_keys(i).start()

    @pl.when(sends_tail)
    def _():
        for head in range(ROWS):
            tail(head).start()

    for j in range(4):
        for i in (2, 1, 3):
            send_values(i, j).start()

    for j in range(4):
        raw[j, spot(h), :] = packed[h, j]
    land[h] = quarter[h]

    for i in (1, 3, 2):
        send_keys(i).wait_recv()
    for r in range(ROWS):
        q = land[r].astype(F32)
        for i in range(4):
            raw[4, 16 + r * BLK + i * 64 : 16 + r * BLK + i * 64 + 64, :] = pltpu.roll(
                q, 96 - 32 * i, 1
            ).astype(BF16)

    @pl.when(c == 0)
    def _():
        raw[:, 0:16, :] = jnp.zeros((TILES, 16, 128), BF16)

    @pl.when(c > 0)
    def _():
        tail(0).wait_recv()

    def gate(j, b, cols):
        v = raw[j, pl.ds(pl.multiple_of(b * BLK, 16), BLK + 16), :].astype(F32)
        t = [tap[i : i + 1, cols] for i in range(3)]
        return (v * (t[0] * v + t[1] * pltpu.roll(v, 1, 0) + t[2] * pltpu.roll(v, 2, 0)))[16:]

    ones = jnp.ones((8, BLK), BF16)
    load_select.wait()
    k1, k2, q1, q2 = (select[i * FP : i * FP + FP] for i in range(4))
    move = select[4 * FP :]

    @pl.loop(0, ROWS)
    def _(b):
        qk = jnp.where(lane == 0, 1.0, gate(4, b, slice(DV, WIN))).astype(BF16)
        gated[pl.ds(pl.multiple_of(b * BLK, BLK), BLK), DV:] = qk
        phi = (dot_nt(k1, qk) * dot_nt(k2, qk)).astype(BF16)
        phik[b] = phi
        totals[b] = jnp.concatenate([dot_nt(ones, phi), jnp.zeros((8, DV - FP), F32)], axis=1)

    feature = lax.broadcasted_iota(jnp.int32, (FS, 128), 0)

    def share(o):
        tile, part_of = lax.rem(lax.div(o, 2), 4), 2 * lax.div(o, 8) + lax.rem(o, 2)
        return (
            pl.ds(pl.multiple_of(part_of * SR, SR), SR),
            pl.ds(pl.multiple_of(tile * SC, SC), SC),
        )

    mine_rows, mine_cols = share(c)

    def to_owner(o, source):
        rows, cols = share(o)
        return pltpu.make_async_remote_copy(
            mine.at[ROWS, rows, cols],
            z1.at[source],
            z1s.at[o],
            z1r.at[source],
            {"ctx": o},
            MESH,
        )

    def from_owner(to, owner):
        return pltpu.make_async_remote_copy(
            z2.at[to], outer.at[mine_rows, mine_cols], z2s.at[to], z2r.at[owner], {"ctx": to}, MESH
        )

    def other(i):
        return lax.rem(c + i, CTX)

    outer[FS:, :] = jnp.zeros((FP - FS, DV), BF16)

    @pl.loop(0, 4)
    def _(j):
        cols = pl.ds(pl.multiple_of(j * 128, 128), 128)
        for i in (1, 3, 2):
            send_values(i, j).wait_recv()
        inner[...] = jnp.zeros((FS, 128), F32)

        @pl.loop(0, ROWS)
        def _(b):
            value = gate(j, b, cols).astype(BF16)
            gated[pl.ds(pl.multiple_of(b * BLK, BLK), BLK), cols] = value
            state = jnp.where(
                feature == PHI, totals[b, 0:1, cols], dot(phik[b, :FS], value)
            )
            before = inner[...]
            mine[b, :, cols] = before.astype(BF16)
            inner[...] = before + state

        mine[ROWS, :, cols] = inner[...].astype(BF16)
        for i in range(4):
            o = 2 * j + 8 * (i // 2) + i % 2

            @pl.when(o != c)
            def _():
                to_owner(o, c).start()

            @pl.when(o == c)
            def _():
                z1[c] = mine[ROWS, mine_rows, mine_cols]

    causal = lax.broadcasted_iota(jnp.int32, (BLK, BLK), 0) >= lax.broadcasted_iota(
        jnp.int32, (BLK, BLK), 1
    )

    @pl.loop(0, ROWS)
    def _(b):
        rows = pl.ds(pl.multiple_of(b * BLK, BLK), BLK)
        qk = gated[rows, DV:]
        value = gated[rows, :DV]
        phi = (dot_nt(qk, q1) * dot_nt(qk, q2)).astype(BF16)
        phiq[rows, :] = phi
        z = dot_nt(dot_nt(qk, move).astype(BF16), qk)
        kern = jnp.where(causal, 1.0 + z + 0.5 * z * z, 0.0).astype(BF16)
        prior = mine[b]
        prior_total = prior[PHI : PHI + 1, :FP].astype(F32)
        num[rows, :] = dot(kern, value) + dot(phi[:, :FS], prior)
        weight_sum = jnp.sum(kern.astype(F32), axis=1, keepdims=True) + jnp.sum(
            phi.astype(F32) * prior_total, axis=1, keepdims=True
        )
        den[rows, :] = jnp.broadcast_to(weight_sum, (BLK, 128))

    @pl.loop(1, CTX)
    def _(i):
        to_owner(c, other(i)).wait_recv()

    run = jnp.zeros((SR, SC), F32)
    for i in range(CTX):
        z2[i] = run.astype(BF16)
        run = run + z1[i].astype(F32)

    @pl.loop(1, CTX)
    def _(i):
        from_owner(other(i), c).start()

    outer[mine_rows, mine_cols] = z2[c]

    @pl.loop(1, CTX)
    def _(i):
        from_owner(c, other(i)).wait_recv()

    load_w.wait()

    def head(by):
        return pl.ds(pl.multiple_of(lax.rem(h + by, ROWS) * DV, DV), DV)

    def begin(k):
        return jnp.where(k == K - 1, BLK - EDGE, jnp.maximum(k * T - (T - EDGE), 0))

    def tokens(k, n):
        return pl.ds(pl.multiple_of(begin(k), EDGE), n)

    def chunk(k, first, n):
        return pl.ds(pl.multiple_of(begin(k) * 4 + first, EDGE), n)

    def ag(k, n, which):
        first, size, of, to = ((0, 4 * n, 0, 1), (0, 4 * n, 0, 3), (0, 2 * n, 3, 1), (2 * n, 2 * n, 1, 3))[which]
        ref = att.at[chunk(k, first, size), head(of)]
        return pltpu.make_async_remote_copy(ref, ref, ags.at[k, which], agr.at[k, which], row(to), MESH)

    def rs(k, n, which):
        a, b, t = pl.ds(0, HALF), pl.ds(HALF, HALF), tokens(k, n)
        j, cols, to_ref, to = (
            (2, a, opp.at[0, t], right),
            (2, b, opp.at[1, t], left),
            (1, b, left_in.at[t, b], right),
            (3, a, right_in.at[t, a], left),
            (1, a, left_in.at[t, a], right),
            (3, b, right_in.at[t, b], left),
        )[which]
        return pltpu.make_async_remote_copy(
            part.at[chunk(k, j * n, n), cols], to_ref, rss.at[k, which], rsr.at[k, which], to, MESH
        )

    outer_total = outer[PHI : PHI + 1, :FP].astype(F32)

    def attend(k, n):
        places = [
            pl.ds(pl.multiple_of(lax.rem(g + j, ROWS) * BLK + begin(k), EDGE), n) for j in range(4)
        ]
        phi = jnp.concatenate([phiq[place, :] for place in places], axis=0)
        top = jnp.concatenate([num[place, :] for place in places], axis=0) + dot(phi, outer[...])
        bottom = jnp.concatenate([den[place, :] for place in places], axis=0)[:, 0:1] + jnp.sum(
            phi.astype(F32) * outer_total, axis=1, keepdims=True
        )
        att[chunk(k, 0, 4 * n), head(0)] = (top / bottom).astype(BF16)
        ag(k, n, 0).start()
        ag(k, n, 1).start()

    def forward(k, n):
        ag(k, n, 0).wait_recv()
        ag(k, n, 2).start()
        ag(k, n, 1).wait_recv()
        ag(k, n, 3).start()

    def project(k, n):
        ag(k, n, 2).wait_recv()
        ag(k, n, 3).wait_recv()
        for half in range(2):
            for m in range(2):
                cols = slice(half * HALF + m * 512, half * HALF + m * 512 + 512)
                p = dot(att[chunk(k, 0, 4 * n), :], w[:, cols])
                own[tokens(k, n), cols] = p[:n]
                part[chunk(k, n, 3 * n), cols] = p[n:].astype(BF16)
            for which in ((0, 3), (1, 2))[half]:
                rs(k, n, which).start()

    def join(k, n):
        for side, j, cols in ((0, 1, slice(0, HALF)), (1, 3, slice(HALF, 2 * HALF))):
            rs(k, n, side).wait_recv()
            rows = chunk(k, j * n, n)
            both = part[rows, cols].astype(F32) + opp[side, tokens(k, n), :].astype(F32)
            part[rows, cols] = both.astype(BF16)
            rs(k, n, 4 + side).start()

    def store(k, n):
        return pltpu.make_async_copy(out.at[tokens(k, n)], out_to.at[tokens(k, n)], os.at[k])

    def finish(k, n):
        for which in range(2, 6):
            rs(k, n, which).wait_recv()
        t = tokens(k, n)
        out[t, :] = (own[t, :] + left_in[t, :].astype(F32) + right_in[t, :].astype(F32)).astype(BF16)
        store(k, n).start()

    def sized(k, stage):
        edge = jnp.logical_or(k == 0, k == K - 1)

        @pl.when(edge)
        def _():
            stage(k, EDGE)

        @pl.when(jnp.logical_not(edge))
        def _():
            stage(k, T)

    @pl.loop(0, K + 5)
    def _(step):
        for stage, late in ((attend, 0), (forward, 1), (project, 2), (join, 3), (finish, 5)):

            @pl.when(jnp.logical_and(step >= late, step < K + late))
            def _():
                sized(step - late, stage)

    for i in (1, 2, 3):
        send_keys(i).wait_send()
        for j in range(4):
            send_values(i, j).wait_send()

    @pl.when(sends_tail)
    def _():
        for one in range(ROWS):
            tail(one).wait_send()

    @pl.loop(1, CTX)
    def _(i):
        to_owner(other(i), c).wait_send()
        from_owner(other(i), c).wait_send()

    def sent(k, n):
        for which in range(4):
            ag(k, n, which).wait_send()
        for which in range(6):
            rs(k, n, which).wait_send()
        store(k, n).wait()

    @pl.loop(0, K)
    def _(k):
        sized(k, sent)


def shards(projected, conv_taps, out_weight):
    select = jnp.asarray(selectors(), BF16)
    hbm = pl.BlockSpec(memory_space=pl.ANY)
    dma = pltpu.SemaphoreType.DMA
    return pl.pallas_call(
        kernel,
        out_shape=jax.ShapeDtypeStruct((BLK, 2048), BF16),
        in_specs=[hbm] * 4,
        out_specs=hbm,
        scratch_shapes=[
            pltpu.VMEM((BLK, ROWS * (2 * FEAT + DV)), BF16),
            pltpu.VMEM((3, ROWS * (2 * FEAT + DV)), F32),
            pltpu.VMEM((4 * FP + 128, 128), BF16),
            pltpu.VMEM((BLK, 2048), BF16),
            pltpu.VMEM((ROWS, TILES, BLK, 128), BF16),
            pltpu.VMEM((ROWS, BLK // 4, 128), BF16),
            pltpu.VMEM((TILES, 16 + TOK, 128), BF16),
            pltpu.VMEM((ROWS, BLK // 4, 128), BF16),
            pltpu.VMEM((8, WIN), F32),
            pltpu.VMEM((TOK, WIN), BF16),
            pltpu.VMEM((ROWS, FP, BLK), BF16),
            pltpu.VMEM((ROWS, 8, DV), F32),
            pltpu.VMEM((TOK, DV), F32),
            pltpu.VMEM((TOK, 128), F32),
            pltpu.VMEM((TOK, FP), BF16),
            pltpu.VMEM((FS, 128), F32),
            pltpu.VMEM((ROWS + 1, FS, DV), BF16),
            pltpu.VMEM((CTX, SR, SC), BF16),
            pltpu.VMEM((CTX, SR, SC), BF16),
            pltpu.VMEM((FP, DV), BF16),
            pltpu.VMEM((2048, 2048), BF16),
            pltpu.VMEM((TOK, 2048), BF16),
            pltpu.VMEM((TOK, 2048), BF16),
            pltpu.VMEM((BLK, 2048), F32),
            pltpu.VMEM((2, BLK, HALF), BF16),
            pltpu.VMEM((BLK, 2048), BF16),
            pltpu.VMEM((BLK, 2048), BF16),
            dma((3,)),
            dma((K,)),
            dma((4, TILES)),
            dma((4, TILES)),
            dma((4,)),
            dma,
            dma,
            dma((CTX,)),
            dma((CTX,)),
            dma((CTX,)),
            dma((CTX,)),
            dma((K, 4)),
            dma((K, 4)),
            dma((K, 6)),
            dma((K, 6)),
        ],
        compiler_params=pltpu.CompilerParams(
            collective_id=0, has_side_effects=True, vmem_limit_bytes=56 * 2**20
        ),
    )(projected, conv_taps, out_weight, select)


def solution(mesh):
    in_specs = (P(("ctx", "row"), "col"), P(None, "col"), P("col", "row"))
    out_specs = P(("ctx", "col"), "row")
    return jax.shard_map(shards, mesh=mesh, in_specs=in_specs, out_specs=out_specs, check_vma=False)
```

```python
import jax
import jax.numpy as jnp
import numpy as np
from jax import lax
from jax.experimental import pallas as pl
from jax.experimental.pallas import tpu as pltpu
from jax.sharding import PartitionSpec as P

MESH = pl.DeviceIdType.MESH
FEAT = 16
DV = 512
PHI = 153
WIN = 640
BLK = 256
ROWS = 4
CTX = 16
TOK = ROWS * BLK
FP = 256
FS = 192
SR, SC = 48, 128
TILES = 5
K = 9
T, EDGE = 32, 16
HALF = 1024
Q0, K0 = 96, 112
F32, BF16 = jnp.float32, jnp.bfloat16
NT = (((1,), (1,)), ((), ()))


def selectors():
    first, second = np.triu_indices(FEAT)
    k1, k2, q1, q2 = (np.zeros((FP, 128), np.float32) for _ in range(4))
    for m in (k1, k2, q1, q2):
        m[0, 0] = 1.0
    for i in range(FEAT):
        k1[1 + i, K0 + i] = 1.0
        k2[1 + i, 0] = 1.0
        q1[1 + i, Q0 + i] = 1.0
        q2[1 + i, 0] = 0.25
    for n, (i, j) in enumerate(zip(first, second)):
        at = 1 + FEAT + n
        k1[at, K0 + i] = 1.0
        k2[at, K0 + j] = 1.0
        q1[at, Q0 + i] = 1.0
        q2[at, Q0 + j] = 1.0 / 32 if i == j else 1.0 / 16
    move = np.zeros((128, 128), np.float32)
    for i in range(FEAT):
        move[K0 + i, Q0 + i] = 0.25
    return np.concatenate([k1, k2, q1, q2, move])


def dot(a, b):
    return jnp.dot(a, b, preferred_element_type=F32)


def dot_nt(a, b):
    return lax.dot_general(a, b, NT, preferred_element_type=F32)


def kernel(
    proj, taps_in, weight, select_in, out_to,
    x, taps, select, out, packed, quarter, raw, land, tap, gated, phik, totals, num, den, phiq,
    inner, mine, z1, z2, outer, w, att, part, own, opp, left_in, right_in,
    ps, os, xs, xr, ts, tr, ws, z1s, z1r, z2s, z2r, ags, agr, rss, rsr,
):
    c, h, g = lax.axis_index("ctx"), lax.axis_index("row"), lax.axis_index("col")

    def at(axis, index, by, n):
        return {axis: lax.rem(index + by, n)}

    def row(by):
        return at("row", h, by, ROWS)

    right, left = at("col", g, 1, 4), at("col", g, 3, 4)
    sends_tail = jnp.logical_and(h == ROWS - 1, c < CTX - 1)

    load_x = pltpu.make_async_copy(proj, x, ps.at[0])
    load_x.start()
    load_taps = pltpu.make_async_copy(taps_in, taps, ps.at[1])
    load_taps.start()
    load_select = pltpu.make_async_copy(select_in, select, ps.at[2])
    load_select.start()
    load_w = pltpu.make_async_copy(weight, w, ws)
    load_w.start()

    bar = pltpu.get_barrier_semaphore()

    def greet(where):
        pl.semaphore_signal(bar, inc=1, device_id=where, device_id_type=MESH)

    @pl.loop(1, CTX)
    def _(i):
        greet(at("ctx", c, i, CTX))

    @pl.when(jnp.logical_and(h != ROWS - 1, c > 0))
    def _():
        greet({"ctx": c - 1, "row": ROWS - 1})

    for i in range(1, ROWS):
        greet(row(i))
    greet(right)
    greet(left)

    lane = lax.broadcasted_iota(jnp.int32, (BLK, 128), 1)
    lane_q = lax.broadcasted_iota(jnp.int32, (BLK // 4, 128), 1)
    load_x.wait()
    for head in range(ROWS):
        y = pltpu.roll(
            x[:, head * DV : head * DV + WIN].astype(F32), WIN - 2 * FEAT * (head + 1), 1
        )
        for j in range(TILES):
            packed[head, j] = y[:, j * 128 : j * 128 + 128].astype(BF16)
        last = y[:, DV:]
        q = jnp.zeros((BLK // 4, 128), F32)
        for i in range(4):
            part_i = pltpu.roll(last[i * 64 : i * 64 + 64], 32 * (i + 1) % 128, 1)
            q = jnp.where(lane_q // 32 == i, part_i, q)
        quarter[head] = q.astype(BF16)
    load_taps.wait()
    window = taps[:, pl.ds(pl.multiple_of(h * DV, DV), WIN)]
    window = jnp.concatenate([window, jnp.zeros((5, WIN), F32)], axis=0)
    tap[...] = pltpu.roll(window, WIN - 2 * FEAT * (h + 1), 1)

    pl.semaphore_wait(bar, ROWS - 1 + CTX - 1 + 2 + jnp.where(sends_tail, ROWS - 1, 0))

    def spot(r):
        return pl.ds(pl.multiple_of(16 + r * BLK, 16), BLK)

    def send_values(i, j):
        return pltpu.make_async_remote_copy(
            packed.at[lax.rem(h + i, ROWS), j], raw.at[j, spot(h)], xs.at[i, j], xr.at[i, j], row(i), MESH
        )

    def send_keys(i):
        return pltpu.make_async_remote_copy(
            quarter.at[lax.rem(h + i, ROWS)], land.at[h], xs.at[i, 4], xr.at[i, 4], row(i), MESH
        )

    def tail(head):
        return pltpu.make_async_remote_copy(
            packed.at[head, :, pl.ds(BLK - 16, 16)],
            raw.at[:, pl.ds(0, 16)],
            ts.at[head],
            tr,
            {"ctx": lax.rem(c + 1, CTX), "row": head},
            MESH,
        )

    for i in (2, 1, 3):
        send_keys(i).start()

    @pl.when(sends_tail)
    def _():
        for head in range(ROWS):
            tail(head).start()

    for j in range(4):
        for i in (2, 1, 3):
            send_values(i, j).start()

    for j in range(4):
        raw[j, spot(h), :] = packed[h, j]
    land[h] = quarter[h]

    for i in (1, 3, 2):
        send_keys(i).wait_recv()
    for r in range(ROWS):
        q = land[r].astype(F32)
        for i in range(4):
            raw[4, 16 + r * BLK + i * 64 : 16 + r * BLK + i * 64 + 64, :] = pltpu.roll(
                q, 96 - 32 * i, 1
            ).astype(BF16)

    @pl.when(c == 0)
    def _():
        raw[:, 0:16, :] = jnp.zeros((TILES, 16, 128), BF16)

    @pl.when(c > 0)
    def _():
        tail(0).wait_recv()

    def gate(j, b, cols):
        v = raw[j, pl.ds(pl.multiple_of(b * BLK, 16), BLK + 16), :].astype(F32)
        t = [tap[i : i + 1, cols] for i in range(3)]
        return (v * (t[0] * v + t[1] * pltpu.roll(v, 1, 0) + t[2] * pltpu.roll(v, 2, 0)))[16:]

    ones = jnp.ones((8, BLK), BF16)
    load_select.wait()
    k1, k2, q1, q2 = (select[i * FP : i * FP + FP] for i in range(4))
    move = select[4 * FP :]

    @pl.loop(0, ROWS)
    def _(b):
        qk = jnp.where(lane == 0, 1.0, gate(4, b, slice(DV, WIN))).astype(BF16)
        gated[pl.ds(pl.multiple_of(b * BLK, BLK), BLK), DV:] = qk
        phi = (dot_nt(k1, qk) * dot_nt(k2, qk)).astype(BF16)
        phik[b] = phi
        totals[b] = jnp.concatenate([dot_nt(ones, phi), jnp.zeros((8, DV - FP), F32)], axis=1)

    feature = lax.broadcasted_iota(jnp.int32, (FS, 128), 0)

    def share(o):
        tile, part_of = lax.rem(lax.div(o, 2), 4), 2 * lax.div(o, 8) + lax.rem(o, 2)
        return (
            pl.ds(pl.multiple_of(part_of * SR, SR), SR),
            pl.ds(pl.multiple_of(tile * SC, SC), SC),
        )

    mine_rows, mine_cols = share(c)

    def to_owner(o, source):
        rows, cols = share(o)
        return pltpu.make_async_remote_copy(
            mine.at[ROWS, rows, cols],
            z1.at[source],
            z1s.at[o],
            z1r.at[source],
            {"ctx": o},
            MESH,
        )

    def from_owner(to, owner):
        return pltpu.make_async_remote_copy(
            z2.at[to], outer.at[mine_rows, mine_cols], z2s.at[to], z2r.at[owner], {"ctx": to}, MESH
        )

    def other(i):
        return lax.rem(c + i, CTX)

    outer[FS:, :] = jnp.zeros((FP - FS, DV), BF16)

    @pl.loop(0, 4)
    def _(j):
        cols = pl.ds(pl.multiple_of(j * 128, 128), 128)
        for i in (1, 3, 2):
            send_values(i, j).wait_recv()
        inner[...] = jnp.zeros((FS, 128), F32)

        @pl.loop(0, ROWS)
        def _(b):
            value = gate(j, b, cols).astype(BF16)
            gated[pl.ds(pl.multiple_of(b * BLK, BLK), BLK), cols] = value
            state = jnp.where(
                feature == PHI, totals[b, 0:1, cols], dot(phik[b, :FS], value)
            )
            before = inner[...]
            mine[b, :, cols] = before.astype(BF16)
            inner[...] = before + state

        mine[ROWS, :, cols] = inner[...].astype(BF16)
        for i in range(4):
            o = 2 * j + 8 * (i // 2) + i % 2

            @pl.when(o != c)
            def _():
                to_owner(o, c).start()

            @pl.when(o == c)
            def _():
                z1[c] = mine[ROWS, mine_rows, mine_cols]

    causal = lax.broadcasted_iota(jnp.int32, (BLK, BLK), 0) >= lax.broadcasted_iota(
        jnp.int32, (BLK, BLK), 1
    )

    @pl.loop(0, ROWS)
    def _(b):
        rows = pl.ds(pl.multiple_of(b * BLK, BLK), BLK)
        qk = gated[rows, DV:]
        value = gated[rows, :DV]
        phi = (dot_nt(qk, q1) * dot_nt(qk, q2)).astype(BF16)
        phiq[rows, :] = phi
        z = dot_nt(dot_nt(qk, move).astype(BF16), qk)
        kern = jnp.where(causal, 1.0 + z + 0.5 * z * z, 0.0).astype(BF16)
        prior = mine[b]
        prior_total = prior[PHI : PHI + 1, :FP].astype(F32)
        num[rows, :] = dot(kern, value) + dot(phi[:, :FS], prior)
        weight_sum = jnp.sum(kern.astype(F32), axis=1, keepdims=True) + jnp.sum(
            phi.astype(F32) * prior_total, axis=1, keepdims=True
        )
        den[rows, :] = jnp.broadcast_to(weight_sum, (BLK, 128))

    @pl.loop(1, CTX)
    def _(i):
        to_owner(c, other(i)).wait_recv()

    run = jnp.zeros((SR, SC), F32)
    for i in range(CTX):
        z2[i] = run.astype(BF16)
        run = run + z1[i].astype(F32)

    @pl.loop(1, CTX)
    def _(i):
        from_owner(other(i), c).start()

    outer[mine_rows, mine_cols] = z2[c]

    @pl.loop(1, CTX)
    def _(i):
        from_owner(c, other(i)).wait_recv()

    load_w.wait()

    def head(by):
        return pl.ds(pl.multiple_of(lax.rem(h + by, ROWS) * DV, DV), DV)

    def begin(k):
        return jnp.where(k == K - 1, BLK - EDGE, jnp.maximum(k * T - (T - EDGE), 0))

    def tokens(k, n):
        return pl.ds(pl.multiple_of(begin(k), EDGE), n)

    def chunk(k, first, n):
        return pl.ds(pl.multiple_of(begin(k) * 4 + first, EDGE), n)

    def ag(k, n, which):
        first, size, of, to = ((0, 4 * n, 0, 1), (0, 4 * n, 0, 3), (0, 2 * n, 3, 1), (2 * n, 2 * n, 1, 3))[which]
        ref = att.at[chunk(k, first, size), head(of)]
        return pltpu.make_async_remote_copy(ref, ref, ags.at[k, which], agr.at[k, which], row(to), MESH)

    def rs(k, n, which):
        a, b, t = pl.ds(0, HALF), pl.ds(HALF, HALF), tokens(k, n)
        j, cols, to_ref, to = (
            (2, a, opp.at[0, t], right),
            (2, b, opp.at[1, t], left),
            (1, b, left_in.at[t, b], right),
            (3, a, right_in.at[t, a], left),
            (1, a, left_in.at[t, a], right),
            (3, b, right_in.at[t, b], left),
        )[which]
        return pltpu.make_async_remote_copy(
            part.at[chunk(k, j * n, n), cols], to_ref, rss.at[k, which], rsr.at[k, which], to, MESH
        )

    outer_total = outer[PHI : PHI + 1, :FP].astype(F32)

    def attend(k, n):
        places = [
            pl.ds(pl.multiple_of(lax.rem(g + j, ROWS) * BLK + begin(k), EDGE), n) for j in range(4)
        ]
        phi = jnp.concatenate([phiq[place, :] for place in places], axis=0)
        top = jnp.concatenate([num[place, :] for place in places], axis=0) + dot(phi, outer[...])
        bottom = jnp.concatenate([den[place, :] for place in places], axis=0)[:, 0:1] + jnp.sum(
            phi.astype(F32) * outer_total, axis=1, keepdims=True
        )
        att[chunk(k, 0, 4 * n), head(0)] = (top / bottom).astype(BF16)
        ag(k, n, 0).start()
        ag(k, n, 1).start()

    def forward(k, n):
        ag(k, n, 0).wait_recv()
        ag(k, n, 2).start()
        ag(k, n, 1).wait_recv()
        ag(k, n, 3).start()

    def project(k, n):
        ag(k, n, 2).wait_recv()
        ag(k, n, 3).wait_recv()
        for half in range(2):
            for m in range(2):
                cols = slice(half * HALF + m * 512, half * HALF + m * 512 + 512)
                p = dot(att[chunk(k, 0, 4 * n), :], w[:, cols])
                own[tokens(k, n), cols] = p[:n]
                part[chunk(k, n, 3 * n), cols] = p[n:].astype(BF16)
            for which in ((0, 3), (1, 2))[half]:
                rs(k, n, which).start()

    def join(k, n):
        for side, j, cols in ((0, 1, slice(0, HALF)), (1, 3, slice(HALF, 2 * HALF))):
            rs(k, n, side).wait_recv()
            rows = chunk(k, j * n, n)
            both = part[rows, cols].astype(F32) + opp[side, tokens(k, n), :].astype(F32)
            part[rows, cols] = both.astype(BF16)
            rs(k, n, 4 + side).start()

    def store(k, n):
        return pltpu.make_async_copy(out.at[tokens(k, n)], out_to.at[tokens(k, n)], os.at[k])

    def finish(k, n):
        for which in range(2, 6):
            rs(k, n, which).wait_recv()
        t = tokens(k, n)
        out[t, :] = (own[t, :] + left_in[t, :].astype(F32) + right_in[t, :].astype(F32)).astype(BF16)
        store(k, n).start()

    def sized(k, stage):
        edge = jnp.logical_or(k == 0, k == K - 1)

        @pl.when(edge)
        def _():
            stage(k, EDGE)

        @pl.when(jnp.logical_not(edge))
        def _():
            stage(k, T)

    @pl.loop(0, K + 5)
    def _(step):
        for stage, late in ((attend, 0), (forward, 1), (project, 2), (join, 3), (finish, 5)):

            @pl.when(jnp.logical_and(step >= late, step < K + late))
            def _():
                sized(step - late, stage)

    for i in (1, 2, 3):
        send_keys(i).wait_send()
        for j in range(4):
            send_values(i, j).wait_send()

    @pl.when(sends_tail)
    def _():
        for one in range(ROWS):
            tail(one).wait_send()

    @pl.loop(1, CTX)
    def _(i):
        to_owner(other(i), c).wait_send()
        from_owner(other(i), c).wait_send()

    def sent(k, n):
        for which in range(4):
            ag(k, n, which).wait_send()
        for which in range(6):
            rs(k, n, which).wait_send()
        store(k, n).wait()

    @pl.loop(0, K)
    def _(k):
        sized(k, sent)


def shards(projected, conv_taps, out_weight):
    select = jnp.asarray(selectors(), BF16)
    hbm = pl.BlockSpec(memory_space=pl.ANY)
    dma = pltpu.SemaphoreType.DMA
    return pl.pallas_call(
        kernel,
        out_shape=jax.ShapeDtypeStruct((BLK, 2048), BF16),
        in_specs=[hbm] * 4,
        out_specs=hbm,
        scratch_shapes=[
            pltpu.VMEM((BLK, ROWS * (2 * FEAT + DV)), BF16),
            pltpu.VMEM((3, ROWS * (2 * FEAT + DV)), F32),
            pltpu.VMEM((4 * FP + 128, 128), BF16),
            pltpu.VMEM((BLK, 2048), BF16),
            pltpu.VMEM((ROWS, TILES, BLK, 128), BF16),
            pltpu.VMEM((ROWS, BLK // 4, 128), BF16),
            pltpu.VMEM((TILES, 16 + TOK, 128), BF16),
            pltpu.VMEM((ROWS, BLK // 4, 128), BF16),
            pltpu.VMEM((8, WIN), F32),
            pltpu.VMEM((TOK, WIN), BF16),
            pltpu.VMEM((ROWS, FP, BLK), BF16),
            pltpu.VMEM((ROWS, 8, DV), F32),
            pltpu.VMEM((TOK, DV), F32),
            pltpu.VMEM((TOK, 128), F32),
            pltpu.VMEM((TOK, FP), BF16),
            pltpu.VMEM((FS, 128), F32),
            pltpu.VMEM((ROWS + 1, FS, DV), BF16),
            pltpu.VMEM((CTX, SR, SC), BF16),
            pltpu.VMEM((CTX, SR, SC), BF16),
            pltpu.VMEM((FP, DV), BF16),
            pltpu.VMEM((2048, 2048), BF16),
            pltpu.VMEM((TOK, 2048), BF16),
            pltpu.VMEM((TOK, 2048), BF16),
            pltpu.VMEM((BLK, 2048), F32),
            pltpu.VMEM((2, BLK, HALF), BF16),
            pltpu.VMEM((BLK, 2048), BF16),
            pltpu.VMEM((BLK, 2048), BF16),
            dma((3,)),
            dma((K,)),
            dma((4, TILES)),
            dma((4, TILES)),
            dma((4,)),
            dma,
            dma,
            dma((CTX,)),
            dma((CTX,)),
            dma((CTX,)),
            dma((CTX,)),
            dma((K, 4)),
            dma((K, 4)),
            dma((K, 6)),
            dma((K, 6)),
        ],
        compiler_params=pltpu.CompilerParams(
            collective_id=0, has_side_effects=True, vmem_limit_bytes=56 * 2**20
        ),
    )(projected, conv_taps, out_weight, select)


def solution(mesh):
    in_specs = (P(("ctx", "row"), "col"), P(None, "col"), P("col", "row"))
    out_specs = P(("ctx", "col"), "row")
    return jax.shard_map(shards, mesh=mesh, in_specs=in_specs, out_specs=out_specs, check_vma=False)
```
